128 devices in a mesh: row: 16 (over y_hi, x, core), col: 8 (over y_lo, z).
Axes of the slice: x: 4, y: 4 (y_hi: 2, y_lo: 2; y = y_hi * 2 + y_lo), z: 4, core: 2. Of those that a mesh axis runs over, the one named last changes fastest.
Arguments:
- pair: float32 [512, 512, 128], P('row', 'col'), may hold values from -6 to 6
- token_mask: int32 [512], replicated, may hold values 0 or 1
- out_proj: float32 [128, 640], replicated, may hold values from -0.5 to 0.5
- out_final: float32 [128, 128], replicated, may hold values from -0.5 to 0.5
- in_proj: float32 [128, 640], replicated, may hold values from -0.5 to 0.5
- in_final: float32 [128, 128], replicated, may hold values from -0.5 to 0.5
Outputs:
- updated: float32 [512, 512, 128], P('row', 'col')
The draws below stay inside these ranges and needn't reach their ends.
All inputs are finite; a program needn't handle non-finite values.
Results may differ from the reference program's by a relative error of at most 0.0065.
Values may be sent and summed in bfloat16 or wider, within the bound.
No kernel may reach another device: no remote copies, remote signals or barrier semaphores. Data moves between devices by JAX's collectives and lax.ppermute only.
A program may use at most 128 MiB of HBM per device.

```python
import jax
import jax.numpy as jnp
from jax import lax

C = 128
HID = 128
TOKENS = 512


def plant(result, stream_key, low, largest):
    extent = result.shape
    place = [jax.random.randint(jax.random.fold_in(stream_key, axis), (), 0, extent[axis]) for axis in range(len(extent))]
    result = result.at[tuple(place)].set(low)
    longest = extent.index(max(extent))
    place[longest] = (place[longest] + 1) % extent[longest]
    return result.at[tuple(place)].set(largest)


def block_scale(key, shape, shards, low, top_value):
    gain, own = 1.0, jax.random.fold_in(key, 6)
    for position, parts in shards:
        heights = jnp.exp(jax.random.uniform(jax.random.fold_in(own, position), (parts,), jnp.float32, low / len(shards), top_value / len(shards)))
        gain = gain * jnp.repeat(heights, shape[position] // parts).reshape([-1 if axis == position else 1 for axis in range(len(shape))])
    return gain


def gaussian(own_key, dims, deviation, reach, pieces=(), kind=jnp.bfloat16):
    level = block_scale(own_key, dims, pieces, -0.22, 0.18) if pieces else 1.0
    entries = jax.random.normal(own_key, dims, jnp.float32) * deviation * level
    return jnp.minimum(jnp.maximum(entries, -reach), reach).astype(kind)


def setup_inputs(seed: int = 0) -> dict:
    key_list = jax.random.split(jax.random.key(seed), 7)
    pair = gaussian(key_list[0], (TOKENS, TOKENS, C), 1.0, 6.0, ((0, 16), (1, 8)), jnp.float32)
    token_mask = plant((jax.random.randint(key_list[1], (TOKENS,), 0, 8) < 7).astype(jnp.int32), jax.random.fold_in(key_list[1], 1), 0, 1)
    out_proj = gaussian(key_list[2], (C, 4 * HID + C), C ** -0.5, 0.5, (), jnp.float32)
    out_final = gaussian(key_list[3], (HID, C), HID ** -0.5, 0.5, (), jnp.float32)
    in_proj = gaussian(key_list[4], (C, 4 * HID + C), C ** -0.5, 0.5, (), jnp.float32)
    in_final = gaussian(key_list[5], (HID, C), HID ** -0.5, 0.5, (), jnp.float32)
    return dict(pair=pair, token_mask=token_mask, out_proj=out_proj, out_final=out_final, in_proj=in_proj, in_final=in_final)


def layer_norm(values):
    centred = values - lax.optimization_barrier(jnp.mean(values, axis=-1, keepdims=True))
    variance = lax.optimization_barrier(jnp.mean(centred * centred, axis=-1, keepdims=True))
    return centred * lax.rsqrt(variance + 1e-05)

def rounded(values):
    return lax.optimization_barrier(values.astype(jnp.bfloat16)).astype(jnp.float32)

def project(pair, pair_mask, weights, hidden):
    linear = jnp.einsum('ijd,de->ije', layer_norm(pair), weights, precision=lax.Precision.HIGHEST)
    left_side = jax.nn.sigmoid(linear[..., hidden:2 * hidden]) * linear[..., :hidden] * pair_mask[..., None]
    right_side = jax.nn.sigmoid(linear[..., 3 * hidden:4 * hidden]) * linear[..., 2 * hidden:3 * hidden] * pair_mask[..., None]
    gating = jax.nn.sigmoid(linear[..., 4 * hidden:])
    return (rounded(left_side), rounded(right_side), gating)

def finish(pair, gating, triangle, final):
    return pair + gating * jnp.einsum('ijh,hd->ijd', layer_norm(triangle), final, precision=lax.Precision.HIGHEST)

def reference(pair, token_mask, out_proj, out_final, in_proj, in_final):
    hidden = out_final.shape[0]
    token_float = token_mask.astype(jnp.float32)
    pair_mask = token_float[:, None] * token_float[None, :]
    left_side, right_side, gating = project(pair, pair_mask, out_proj, hidden)
    triangle = jnp.einsum('ikc,jkc->ijc', left_side, right_side, precision=lax.Precision.HIGHEST)
    first = finish(pair, gating, triangle, out_final)
    left_side, right_side, gating = project(first, pair_mask, in_proj, hidden)
    triangle = jnp.einsum('kic,kjc->ijc', left_side, right_side, precision=lax.Precision.HIGHEST)
    return finish(first, gating, triangle, in_final)
```

```python
import functools

import jax
import jax.numpy as jnp
from jax import lax
from jax.experimental import pallas as pl
from jax.experimental.pallas import tpu as pltpu
from jax.sharding import PartitionSpec as P

HALF = 64
TILES = 16
F32 = jnp.float32
BF16 = jnp.bfloat16
VMEM = pl.BlockSpec(memory_space=pltpu.VMEM)
SMEM = pl.BlockSpec(memory_space=pltpu.SMEM)


def call(kernel, outs, scratch, specs, flops):
    return pl.pallas_call(
        kernel,
        out_shape=outs,
        in_specs=specs,
        out_specs=jax.tree.map(lambda _: VMEM, outs),
        scratch_shapes=scratch,
        compiler_params=pltpu.CompilerParams(vmem_limit_bytes=48 * 1024 * 1024),
        cost_estimate=pl.CostEstimate(flops=flops, bytes_accessed=3 << 20, transcendentals=1 << 19),
    )


def low_lanes(shape):
    return lax.broadcasted_iota(jnp.int32, shape, len(shape) - 1) < HALF


def turn(values):
    return pltpu.roll(values, HALF, axis=values.ndim - 1)


def gate(values):
    return 0.5 * jnp.tanh(0.5 * values) + 0.5


def norm(values):
    scale = 1.0 / values.shape[0]
    centred = values - jnp.sum(values, axis=0, keepdims=True) * scale
    variance = jnp.sum(centred * centred, axis=0, keepdims=True) * scale
    return centred * lax.rsqrt(variance + 1e-05)


def dot(left, right, dims=((1,), (0,))):
    return lax.dot_general(left, right, (dims, ((), ())), preferred_element_type=F32)


def transposed(weights, start, stop):
    parts = [weights[:, k : k + 128].T for k in range(start, stop, 128)]
    return jnp.concatenate(parts, axis=0).astype(BF16)


def masks(token_s, token_v):
    row = lax.axis_index("row")
    col = lax.axis_index("col")
    line = token_v[pl.ds(col // 2, 1), :].astype(F32)
    low = low_lanes((1, 128))
    odd = col % 2
    pick = jnp.where(low, 1, 0) != odd
    cols = jnp.where(pick, line, turn(line))

    def of_tile(tile):
        first = row * 32 + (tile // 8) * 16 + tile % 8
        top = token_s[first].astype(F32)
        bottom = token_s[first + 8].astype(F32)
        return cols * jnp.where(low, top, bottom)

    return of_tile


def pair_tile(pair, tile):
    first = (tile // 8) * 16 + tile % 8
    return jnp.concatenate([pair[first], pair[first + 8]], axis=0).T


def sides(normed, weights, mask, low, held, slot):
    linear = dot(weights, normed)
    left = gate(linear[128:256]) * linear[0:128] * mask
    right = gate(linear[384:512]) * linear[256:384] * mask
    for k in range(2):
        lanes = slice(128 * k, 128 * (k + 1))
        held[slot + k] = jnp.where(low, left[:, lanes], turn(right[:, lanes]))
        held[slot + k + 8] = jnp.where(low, turn(left[:, lanes]), right[:, lanes])


def pack(held, out, group):
    for k in range(0, 128, 32):
        out[k : k + 32, 16 * group : 16 * group + 16, :] = jnp.swapaxes(held[:, k : k + 32, :], 0, 1).astype(BF16)


def project_kernel(token_s, token_v, pair, proj, out, held):
    weights = transposed(proj, 0, 512)
    of_tile = masks(token_s, token_v)
    low = low_lanes((128, 128))
    for group in range(2):
        for slot in range(0, 8, 2):
            tile = 8 * group + slot
            mask = jnp.concatenate([of_tile(tile), of_tile(tile + 1)], axis=1)
            values = jnp.concatenate([pair_tile(pair, tile), pair_tile(pair, tile + 1)], axis=1)
            sides(norm(values).astype(BF16), weights, mask, low, held, slot)
        pack(held, out, group)


def gating_kernel(pair, proj, flat, gating):
    weights = transposed(proj, 512, 640)
    for tile in range(0, TILES, 2):
        values = jnp.concatenate([pair_tile(pair, tile), pair_tile(pair, tile + 1)], axis=1)
        lanes = slice(128 * tile, 128 * (tile + 2))
        flat[:, lanes] = values
        gating[:, lanes] = gate(dot(weights, norm(values).astype(BF16)))


def operands(got, left, right):
    for k in range(4):
        lanes = slice(128 * k, 128 * (k + 1))
        even = got[:, 2 * k].reshape(512, 128)
        odd = got[:, 2 * k + 1].reshape(512, 128)
        left[:, lanes] = jnp.concatenate([even[:, :HALF], odd[:, :HALF]], axis=1)
        right[:, lanes] = jnp.concatenate([even[:, HALF:], odd[:, HALF:]], axis=1)


def triangle_kernel(contract, got, out, left, right):
    operands(got, left, right)
    low = low_lanes((16, 128))
    for k in range(0, 16, 4):
        rows = slice(32 * k, 32 * (k + 4))
        if contract == 1:
            sums = dot(left[rows, :], right[...], ((1,), (1,)))
        else:
            sums = dot(left[:, rows], right[...], ((0,), (0,)))
        sums = sums.reshape(4, 2, 2, 8, 512)
        for n in range(4):
            for m in range(4):
                lanes = slice(128 * m, 128 * (m + 1))
                top = sums[n, :, 0, :, lanes].reshape(16, 128)
                bottom = sums[n, :, 1, :, lanes].reshape(16, 128)
                out[k + n, 2 * m] = jnp.where(low, top, turn(bottom)).astype(BF16)
                out[k + n, 2 * m + 1] = jnp.where(low, turn(top), bottom).astype(BF16)


def unpack(got, held):
    for k in range(0, 128, 32):
        held[:, k : k + 32, :] = jnp.swapaxes(got[k : k + 32].astype(F32), 0, 1)


def middle_kernel(token_s, token_v, got, flat, gating, final, proj, out, first, held, triangle):
    weights = transposed(proj, 0, 512)
    closing = transposed(final, 0, 128)
    of_tile = masks(token_s, token_v)
    low = low_lanes((128, 128))
    unpack(got, triangle)
    for group in range(2):
        for slot in range(0, 8, 2):
            tile = 8 * group + slot
            lanes = slice(128 * tile, 128 * (tile + 2))
            mask = jnp.concatenate([of_tile(tile), of_tile(tile + 1)], axis=1)
            values = norm(jnp.concatenate([triangle[tile], triangle[tile + 1]], axis=1)).astype(BF16)
            values = flat[:, lanes] + gating[:, lanes] * dot(closing, values)
            first[:, lanes] = values
            sides(norm(values).astype(BF16), weights, mask, low, held, slot)
        pack(held, out, group)


def second_gating_kernel(first, proj, turned, gating):
    weights = proj[:, 512:640].astype(BF16)
    for tile in range(TILES):
        values = first[:, 128 * tile : 128 * (tile + 1)]
        turned[tile] = values.T
        gating[tile] = gate(dot(norm(values).astype(BF16), weights, ((0,), (0,))))


def last_kernel(got, turned, gating, final, out, triangle):
    closing = final[...].astype(BF16)
    unpack(got, triangle)
    for tile in range(TILES):
        row = (tile // 8) * 16 + tile % 8
        values = turned[tile] + gating[tile] * dot(norm(triangle[tile]).astype(BF16), closing, ((0,), (0,)))
        out[row] = values[:HALF]
        out[row + 8] = values[HALF:]


def shards(pair, token_mask, out_proj, out_final, in_proj, in_final):
    axes = ("row", "col")
    struct = jax.ShapeDtypeStruct
    lines = token_mask.reshape(4, 128)
    message = struct((128, 32, 128), BF16)
    answer = struct((16, 8, 16, 128), BF16)
    whole = struct((128, 2048), F32)
    held = pltpu.VMEM((16, 128, 128), F32)
    operand = pltpu.VMEM((512, 512), BF16)

    def swap(values):
        return lax.all_to_all(values, axes, 0, 0, tiled=True)

    def triangle(got, contract):
        kernel = functools.partial(triangle_kernel, contract)
        sums = call(kernel, answer, [operand, operand], [VMEM], 2 * 512**3)(got.reshape(16, 8, 32, 128))
        return sums.reshape(128, 16, 128)

    sent = call(project_kernel, message, [held], [SMEM, VMEM, VMEM, VMEM], 2 * 2048 * 128 * 512)(
        token_mask, lines, pair, out_proj
    )
    flat, gating = call(gating_kernel, (whole, whole), [], [VMEM, VMEM], 2 * 2048 * 128 * 128)(pair, out_proj)
    sums = swap(triangle(swap(sent), 1))
    sent, first = call(
        middle_kernel, (message, whole), [held, held], [SMEM] + [VMEM] * 6, 2 * 2048 * 128 * 640
    )(token_mask, lines, sums, flat, gating, out_final, in_proj)
    tiles = struct((TILES, 128, 128), F32)
    turned, gating = call(second_gating_kernel, (tiles, tiles), [], [VMEM, VMEM], 2 * 2048 * 128 * 128)(first, in_proj)
    sums = swap(triangle(swap(sent), 0))
    return call(last_kernel, struct(pair.shape, F32), [held], [VMEM] * 4, 2 * 2048 * 128 * 128)(
        sums, turned, gating, in_final
    )


def solution(mesh):
    placed = (P("row", "col", None), P(), P(), P(), P(), P())
    return jax.shard_map(
        shards, mesh=mesh, in_specs=placed, out_specs=P("row", "col", None), check_vma=False
    )
```

```python
import functools

import jax
import jax.numpy as jnp
from jax import lax
from jax.experimental import pallas as pl
from jax.experimental.pallas import tpu as pltpu
from jax.sharding import PartitionSpec as P

HALF = 64
TILES = 16
F32 = jnp.float32
BF16 = jnp.bfloat16
VMEM = pl.BlockSpec(memory_space=pltpu.VMEM)
SMEM = pl.BlockSpec(memory_space=pltpu.SMEM)
HBM = pl.BlockSpec(memory_space=pltpu.HBM)


def call(kernel, outs, scratch, specs, flops, limit=16):
    return pl.pallas_call(
        kernel,
        out_shape=outs,
        in_specs=specs,
        out_specs=jax.tree.map(lambda _: VMEM, outs),
        scratch_shapes=scratch,
        compiler_params=pltpu.CompilerParams(vmem_limit_bytes=limit * 1024 * 1024),
        cost_estimate=pl.CostEstimate(flops=flops, bytes_accessed=3 << 20, transcendentals=1 << 19),
    )


def low_lanes(shape):
    return lax.broadcasted_iota(jnp.int32, shape, len(shape) - 1) < HALF


def turn(values):
    return pltpu.roll(values, HALF, axis=values.ndim - 1)


def norm(values, mask=None):
    scale = 1.0 / values.shape[0]
    centred = values - jnp.sum(values, axis=0, keepdims=True) * scale
    factor = lax.rsqrt(jnp.sum(centred * centred, axis=0, keepdims=True) * scale + 1e-05)
    return centred * (factor if mask is None else factor * mask)


def dot(left, right, dims=((1,), (0,))):
    return lax.dot_general(left, right, (dims, ((), ())), preferred_element_type=F32)


def halved(weights):
    parts = [weights[:, k : k + 128].T for k in range(0, weights.shape[1], 128)]
    return (jnp.concatenate(parts, axis=0) * 0.5).astype(BF16)


def masks(token_s, token_v):
    row = lax.axis_index("row")
    col = lax.axis_index("col")
    line = token_v[pl.ds(col // 2, 1), :].astype(F32)
    low = low_lanes((1, 128))
    odd = col % 2
    pick = jnp.where(low, 1, 0) != odd
    cols = jnp.where(pick, line, turn(line))

    def of_tile(tile):
        first = row * 32 + (tile // 8) * 16 + tile % 8
        top = token_s(first).astype(F32)
        bottom = token_s(first + 8).astype(F32)
        return cols * jnp.where(low, top, bottom)

    return lambda tile: jnp.concatenate([of_tile(tile), of_tile(tile + 1)], axis=1)


def pair_tile(pair, tile):
    first = (tile // 8) * 16 + tile % 8
    return jnp.concatenate([pair[first], pair[first + 8]], axis=0).T


def sides(normed, weights, held, slot):
    linear = dot(weights, normed.astype(BF16))
    left = ((1.0 + jnp.tanh(linear[128:256])) * linear[0:128]).astype(BF16)
    right = ((1.0 + jnp.tanh(linear[384:512])) * linear[256:384]).astype(BF16)
    for k in range(2):
        low = slice(128 * k, 128 * k + HALF)
        high = slice(128 * k + HALF, 128 * (k + 1))
        held[slot + k] = jnp.concatenate([left[:, low], right[:, low]], axis=1)
        held[slot + k + 8] = jnp.concatenate([left[:, high], right[:, high]], axis=1)
    return 1.0 + jnp.tanh(linear[512:640])


def pack(held, out, group):
    for k in range(0, 128, 32):
        out[k : k + 32, 16 * group : 16 * group + 16, :] = jnp.swapaxes(held[:, k : k + 32, :], 0, 1)


def project_kernel(
    token_h, pair_h, proj_h, out, flat, gating, held, token_s, token_v, pair, proj, semaphores
):
    rows = [(8 * k + 4 * part, 4) for k in (0, 2) for part in (0, 1)]
    rows = [(first + step, 4) for first, _ in rows for step in (0, 8)]
    copies = [
        pltpu.make_async_copy(pair_h.at[pl.ds(first, n)], pair.at[pl.ds(first, n)], semaphores.at[k])
        for k, (first, n) in enumerate(rows)
    ]
    others = [
        pltpu.make_async_copy(proj_h, proj, semaphores.at[8]),
        pltpu.make_async_copy(token_h, token_s, semaphores.at[9]),
        pltpu.make_async_copy(token_h, token_v, semaphores.at[10]),
    ]
    for copy in others + copies:
        copy.start()
    others[0].wait()
    weights = halved(proj)
    others[1].wait()
    others[2].wait()
    mask = masks(lambda n: token_s[n // 128, n % 128], token_v)
    for group in range(2):
        for slot in range(0, 8, 2):
            if slot % 4 == 0:
                for copy in copies[4 * group + slot // 2 : 4 * group + slot // 2 + 2]:
                    copy.wait()
            tile = 8 * group + slot
            lanes = slice(128 * tile, 128 * (tile + 2))
            values = jnp.concatenate([pair_tile(pair, tile), pair_tile(pair, tile + 1)], axis=1)
            flat[:, lanes] = values
            gating[:, lanes] = sides(norm(values, mask(tile)), weights, held, slot)
        pack(held, out, group)


def operands(got, left, right):
    for k in range(4):
        lanes = slice(128 * k, 128 * (k + 1))
        even = got[:, 2 * k].reshape(512, 128)
        odd = got[:, 2 * k + 1].reshape(512, 128)
        left[:, lanes] = jnp.concatenate([even[:, :HALF], odd[:, :HALF]], axis=1)
        right[:, lanes] = jnp.concatenate([even[:, HALF:], odd[:, HALF:]], axis=1)


def triangle_kernel(contract, got, out, left, right):
    operands(got, left, right)
    low = low_lanes((16, 128))
    for k in range(0, 16, 4):
        rows = slice(32 * k, 32 * (k + 4))
        if contract == 1:
            sums = dot(left[rows, :], right[...], ((1,), (1,)))
        else:
            sums = dot(left[:, rows], right[...], ((0,), (0,)))
        sums = sums.reshape(4, 2, 2, 8, 512)
        for n in range(4):
            for m in range(4):
                lanes = slice(128 * m, 128 * (m + 1))
                top = sums[n, :, 0, :, lanes].reshape(16, 128)
                bottom = sums[n, :, 1, :, lanes].reshape(16, 128)
                out[k + n, 2 * m] = jnp.where(low, top, turn(bottom)).astype(BF16)
                out[k + n, 2 * m + 1] = jnp.where(low, turn(top), bottom).astype(BF16)


def unpack(got, triangle):
    for k in range(0, 128, 32):
        triangle[:, k : k + 32, :] = jnp.swapaxes(got[k : k + 32], 0, 1)


def finish(triangle, tile, flat, gating, closing):
    lanes = slice(128 * tile, 128 * (tile + 2))
    sums = jnp.concatenate([triangle[tile], triangle[tile + 1]], axis=1).astype(F32)
    return flat[:, lanes] + gating[:, lanes] * dot(closing, norm(sums).astype(BF16))


def middle_kernel(
    token_s, token_v, got, flat, gating, final, proj, out, first, next_gating, held, triangle
):
    weights = halved(proj)
    closing = halved(final)
    mask = masks(lambda n: token_s[n // 128, n % 128], token_v)
    unpack(got, triangle)
    for group in range(2):
        for slot in range(0, 8, 2):
            tile = 8 * group + slot
            lanes = slice(128 * tile, 128 * (tile + 2))
            values = finish(triangle, tile, flat, gating, closing)
            first[:, lanes] = values
            next_gating[:, lanes] = sides(norm(values, mask(tile)), weights, held, slot)
        pack(held, out, group)


def last_kernel(got, first, gating, final, out, triangle, done, semaphores):
    closing = halved(final)
    unpack(got, triangle)
    copies = []
    for tile in range(0, TILES, 2):
        values = finish(triangle, tile, first, gating, closing)
        row = (tile // 8) * 16 + tile % 8
        for k in range(2):
            part = values[:, 128 * k : 128 * (k + 1)].T
            done[row + k] = part[:HALF]
            done[row + k + 8] = part[HALF:]
        if tile % 4 == 2:
            for start in (row - 2, row + 6):
                copies.append(
                    pltpu.make_async_copy(
                        done.at[pl.ds(start, 4)], out.at[pl.ds(start, 4)], semaphores.at[len(copies)]
                    )
                )
                copies[-1].start()
    for copy in copies:
        copy.wait()


def shards(pair, token_mask, out_proj, out_final, in_proj, in_final):
    axes = ("row", "col")
    struct = jax.ShapeDtypeStruct
    lines = token_mask.reshape(4, 128)
    message = struct((128, 32, 128), BF16)
    answer = struct((16, 8, 16, 128), BF16)
    whole = struct((128, 2048), F32)
    held = pltpu.VMEM((16, 128, 128), BF16)
    operand = pltpu.VMEM((512, 512), BF16)

    def swap(values):
        return lax.all_to_all(values, axes, 0, 0, tiled=True)

    def triangle(got, contract):
        kernel = functools.partial(triangle_kernel, contract)
        sums = call(kernel, answer, [operand, operand], [VMEM], 2 * 512**3)(got.reshape(16, 8, 32, 128))
        return sums.reshape(128, 16, 128)

    scratch = [
        held,
        pltpu.SMEM((4, 128), jnp.int32),
        pltpu.VMEM((4, 128), jnp.int32),
        pltpu.VMEM(pair.shape, F32),
        pltpu.VMEM(out_proj.shape, F32),
        pltpu.SemaphoreType.DMA((11,)),
    ]
    sent, flat, gating = call(
        project_kernel, (message, whole, whole), scratch, [HBM] * 3, 2 * 2048 * 128 * 640
    )(*[pltpu.with_memory_space_constraint(v, pltpu.HBM) for v in (lines, pair, out_proj)])
    sums = swap(triangle(swap(sent), 1))
    sent, first, gating = call(
        middle_kernel, (message, whole, whole), [held, held], [SMEM] + [VMEM] * 6, 2 * 2048 * 128 * 768
    )(lines, lines, sums, flat, gating, out_final, in_proj)
    sums = swap(triangle(swap(sent), 0))
    return pl.pallas_call(
        last_kernel,
        out_shape=struct(pair.shape, F32),
        in_specs=[VMEM] * 4,
        out_specs=HBM,
        scratch_shapes=[held, pltpu.VMEM(pair.shape, F32), pltpu.SemaphoreType.DMA((8,))],
        compiler_params=pltpu.CompilerParams(vmem_limit_bytes=16 * 1024 * 1024),
        cost_estimate=pl.CostEstimate(flops=2 * 2048 * 128 * 128, bytes_accessed=3 << 20, transcendentals=0),
    )(sums, first, gating, in_final)


def solution(mesh):
    placed = (P("row", "col", None), P(), P(), P(), P(), P())
    return jax.shard_map(
        shards, mesh=mesh, in_specs=placed, out_specs=P("row", "col", None), check_vma=False
    )
```

```python
import functools

import jax
import jax.numpy as jnp
from jax import lax
from jax.experimental import pallas as pl
from jax.experimental.pallas import tpu as pltpu
from jax.sharding import PartitionSpec as P

HALF = 64
TILES = 16
F32 = jnp.float32
BF16 = jnp.bfloat16
VMEM = pl.BlockSpec(memory_space=pltpu.VMEM)
SMEM = pl.BlockSpec(memory_space=pltpu.SMEM)
HBM = pl.BlockSpec(memory_space=pltpu.HBM)


def call(kernel, outs, scratch, specs, flops, limit=16):
    return pl.pallas_call(
        kernel,
        out_shape=outs,
        in_specs=specs,
        out_specs=jax.tree.map(lambda _: VMEM, outs),
        scratch_shapes=scratch,
        compiler_params=pltpu.CompilerParams(vmem_limit_bytes=limit * 1024 * 1024),
        cost_estimate=pl.CostEstimate(flops=flops, bytes_accessed=3 << 20, transcendentals=1 << 19),
    )


def low_lanes(shape):
    return lax.broadcasted_iota(jnp.int32, shape, len(shape) - 1) < HALF


def turn(values):
    return pltpu.roll(values, HALF, axis=values.ndim - 1)


def norm(values, mask=None):
    scale = 1.0 / values.shape[0]
    centred = values - jnp.sum(values, axis=0, keepdims=True) * scale
    factor = lax.rsqrt(jnp.sum(centred * centred, axis=0, keepdims=True) * scale + 1e-05)
    return centred * (factor if mask is None else factor * mask)


def dot(left, right, dims=((1,), (0,))):
    return lax.dot_general(left, right, (dims, ((), ())), preferred_element_type=F32)


def halved(weights):
    parts = [weights[:, k : k + 128].T for k in range(0, weights.shape[1], 128)]
    return (jnp.concatenate(parts, axis=0) * 0.5).astype(BF16)


def masks(tokens):
    row = lax.axis_index("row")
    col = lax.axis_index("col")
    line = tokens[pl.ds(col // 2, 1), :].astype(F32)
    pick = jnp.where(low_lanes((1, 128)), 1, 0) != col % 2
    cols = jnp.where(pick, line, turn(line))
    line = jnp.broadcast_to(tokens[pl.ds(row // 4, 1), :].astype(F32), (32, 128))
    lane = lax.broadcasted_iota(jnp.int32, (32, 128), 1)
    own = lax.broadcasted_iota(jnp.int32, (32, 128), 0) + 32 * (row % 4)
    rows = jnp.sum(jnp.where(lane == own, line, 0.0), axis=1, keepdims=True) * cols
    low = low_lanes((8, 128))
    return jnp.concatenate([jnp.where(low, rows[k : k + 8], rows[k + 8 : k + 16]) for k in (0, 16)], axis=0)


def mask_of(mask, tile):
    return jnp.concatenate([mask[tile : tile + 1], mask[tile + 1 : tile + 2]], axis=1)


def pair_tile(pair, tile):
    place = (tile // 8, slice(None), tile % 8 // 4, tile % 4)
    return pair[place].reshape(128, 128).T


def sides(normed, weights, held, slot):
    linear = dot(weights, normed.astype(BF16))
    left = ((1.0 + jnp.tanh(linear[128:256])) * linear[0:128]).astype(BF16)
    right = ((1.0 + jnp.tanh(linear[384:512])) * linear[256:384]).astype(BF16)
    for k in range(2):
        low = slice(128 * k, 128 * k + HALF)
        high = slice(128 * k + HALF, 128 * (k + 1))
        held[slot + k] = jnp.concatenate([left[:, low], right[:, low]], axis=1)
        held[slot + k + 8] = jnp.concatenate([left[:, high], right[:, high]], axis=1)
    return 1.0 + jnp.tanh(linear[512:640])


def pack(held, out, group):
    for k in range(0, 128, 32):
        out[k : k + 32, 16 * group : 16 * group + 16, :] = jnp.swapaxes(held[:, k : k + 32, :], 0, 1)


def project_kernel(token_h, pair_h, proj_h, out, flat, gating, mask, held, tokens, pair, proj, semaphores):
    parts = [(group, slice(None), part) for group in (0, 1) for part in (0, 1)]
    copies = [
        pltpu.make_async_copy(pair_h.at[part], pair.at[part], semaphores.at[k])
        for k, part in enumerate(parts)
    ]
    weight_copy = pltpu.make_async_copy(proj_h, proj, semaphores.at[4])
    token_copy = pltpu.make_async_copy(token_h, tokens, semaphores.at[5])
    for copy in [weight_copy, token_copy] + copies:
        copy.start()
    for copy in copies:
        copy.wait()
    weight_copy.wait()
    token_copy.wait()
    weights = halved(proj)
    mask[...] = masks(tokens)
    for group in range(2):
        for slot in range(0, 8, 2):
            tile = 8 * group + slot
            lanes = slice(128 * tile, 128 * (tile + 2))
            values = jnp.concatenate([pair_tile(pair, tile), pair_tile(pair, tile + 1)], axis=1)
            flat[:, lanes] = values
            gating[:, lanes] = sides(norm(values, mask_of(mask, tile)), weights, held, slot)
        pack(held, out, group)


def operands(got, left, right):
    for k in range(4):
        lanes = slice(128 * k, 128 * (k + 1))
        even = got[:, 2 * k].reshape(512, 128)
        odd = got[:, 2 * k + 1].reshape(512, 128)
        left[:, lanes] = jnp.concatenate([even[:, :HALF], odd[:, :HALF]], axis=1)
        right[:, lanes] = jnp.concatenate([even[:, HALF:], odd[:, HALF:]], axis=1)


def triangle_kernel(contract, got, out, left, right):
    operands(got, left, right)
    low = low_lanes((16, 128))
    for k in range(0, 16, 4):
        rows = slice(32 * k, 32 * (k + 4))
        if contract == 1:
            sums = dot(left[rows, :], right[...], ((1,), (1,)))
        else:
            sums = dot(left[:, rows], right[...], ((0,), (0,)))
        sums = sums.reshape(4, 2, 2, 8, 512)
        for n in range(4):
            for m in range(4):
                lanes = slice(128 * m, 128 * (m + 1))
                top = sums[n, :, 0, :, lanes].reshape(16, 128)
                bottom = sums[n, :, 1, :, lanes].reshape(16, 128)
                out[k + n, 2 * m] = jnp.where(low, top, turn(bottom)).astype(BF16)
                out[k + n, 2 * m + 1] = jnp.where(low, turn(top), bottom).astype(BF16)


def unpack(got, triangle):
    for k in range(0, 128, 32):
        triangle[:, k : k + 32, :] = jnp.swapaxes(got[k : k + 32], 0, 1)


def finish(triangle, tile, flat, gating, closing):
    lanes = slice(128 * tile, 128 * (tile + 2))
    sums = jnp.concatenate([triangle[tile], triangle[tile + 1]], axis=1).astype(F32)
    return flat[:, lanes] + gating[:, lanes] * dot(closing, norm(sums).astype(BF16))


def middle_kernel(
    mask, got, flat, gating, final, proj, out, first, next_gating, held, triangle
):
    weights = halved(proj)
    closing = halved(final)
    unpack(got, triangle)
    for group in range(2):
        for slot in range(0, 8, 2):
            tile = 8 * group + slot
            lanes = slice(128 * tile, 128 * (tile + 2))
            values = finish(triangle, tile, flat, gating, closing)
            first[:, lanes] = values
            next_gating[:, lanes] = sides(norm(values, mask_of(mask, tile)), weights, held, slot)
        pack(held, out, group)


def last_kernel(got, first, gating, final, out, triangle, done, semaphores):
    closing = halved(final)
    unpack(got, triangle)
    copies = []
    for tile in range(0, TILES, 2):
        values = finish(triangle, tile, first, gating, closing)
        row = (tile // 8) * 16 + tile % 8
        for k in range(2):
            part = values[:, 128 * k : 128 * (k + 1)].T
            done[row + k] = part[:HALF]
            done[row + k + 8] = part[HALF:]
        if tile % 4 == 2:
            for start in (row - 2, row + 6):
                copies.append(
                    pltpu.make_async_copy(
                        done.at[pl.ds(start, 4)], out.at[pl.ds(start, 4)], semaphores.at[len(copies)]
                    )
                )
                copies[-1].start()
    for copy in copies:
        copy.wait()


def shards(pair, token_mask, out_proj, out_final, in_proj, in_final):
    axes = ("row", "col")
    struct = jax.ShapeDtypeStruct
    lines = token_mask.reshape(4, 128)
    message = struct((128, 32, 128), BF16)
    answer = struct((16, 8, 16, 128), BF16)
    whole = struct((128, 2048), F32)
    held = pltpu.VMEM((16, 128, 128), BF16)
    operand = pltpu.VMEM((512, 512), BF16)

    def swap(values):
        return lax.all_to_all(values, axes, 0, 0, tiled=True)

    def triangle(got, contract):
        kernel = functools.partial(triangle_kernel, contract)
        sums = call(kernel, answer, [operand, operand], [VMEM], 2 * 512**3)(got.reshape(16, 8, 32, 128))
        return sums.reshape(128, 16, 128)

    scratch = [
        held,
        pltpu.VMEM((4, 128), jnp.int32),
        pltpu.VMEM((2, 2, 2, 4, 64, 128), F32),
        pltpu.VMEM(out_proj.shape, F32),
        pltpu.SemaphoreType.DMA((6,)),
    ]
    sent, flat, gating, mask = call(
        project_kernel, (message, whole, whole, struct((TILES, 128), F32)), scratch, [HBM] * 3, 2 * 2048 * 128 * 640
    )(*[pltpu.with_memory_space_constraint(v, pltpu.HBM) for v in (lines, pair.reshape(2, 2, 2, 4, 64, 128), out_proj)])
    sums = swap(triangle(swap(sent), 1))
    sent, first, gating = call(
        middle_kernel, (message, whole, whole), [held, held], [VMEM] * 6, 2 * 2048 * 128 * 768
    )(mask, sums, flat, gating, out_final, in_proj)
    sums = swap(triangle(swap(sent), 0))
    return pl.pallas_call(
        last_kernel,
        out_shape=struct(pair.shape, F32),
        in_specs=[VMEM] * 4,
        out_specs=HBM,
        scratch_shapes=[held, pltpu.VMEM(pair.shape, F32), pltpu.SemaphoreType.DMA((8,))],
        compiler_params=pltpu.CompilerParams(vmem_limit_bytes=16 * 1024 * 1024),
        cost_estimate=pl.CostEstimate(flops=2 * 2048 * 128 * 128, bytes_accessed=3 << 20, transcendentals=0),
    )(sums, first, gating, in_final)


def solution(mesh):
    placed = (P("row", "col", None), P(), P(), P(), P(), P())
    return jax.shard_map(
        shards, mesh=mesh, in_specs=placed, out_specs=P("row", "col", None), check_vma=False
    )
```

```python
import functools

import jax
import jax.numpy as jnp
from jax import lax
from jax.experimental import pallas as pl
from jax.experimental.pallas import tpu as pltpu
from jax.sharding import PartitionSpec as P

HALF = 64
TILES = 16
F32 = jnp.float32
BF16 = jnp.bfloat16
VMEM = pl.BlockSpec(memory_space=pltpu.VMEM)
SMEM = pl.BlockSpec(memory_space=pltpu.SMEM)
HBM = pl.BlockSpec(memory_space=pltpu.HBM)


def call(kernel, outs, scratch, specs, flops, limit=16):
    return pl.pallas_call(
        kernel,
        out_shape=outs,
        in_specs=specs,
        out_specs=jax.tree.map(lambda _: VMEM, outs),
        scratch_shapes=scratch,
        compiler_params=pltpu.CompilerParams(vmem_limit_bytes=limit * 1024 * 1024),
        cost_estimate=pl.CostEstimate(flops=flops, bytes_accessed=3 << 20, transcendentals=1 << 19),
    )


def low_lanes(shape):
    return lax.broadcasted_iota(jnp.int32, shape, len(shape) - 1) < HALF


def turn(values):
    return pltpu.roll(values, HALF, axis=values.ndim - 1)


def norm(values, mask=None):
    scale = 1.0 / values.shape[0]
    centred = values - jnp.sum(values, axis=0, keepdims=True) * scale
    factor = lax.rsqrt(jnp.sum(centred * centred, axis=0, keepdims=True) * scale + 1e-05)
    return centred * (factor if mask is None else factor * mask)


def dot(left, right, dims=((1,), (0,))):
    return lax.dot_general(left, right, (dims, ((), ())), preferred_element_type=F32)


def halved(weights):
    parts = [weights[:, k : k + 128].T for k in range(0, weights.shape[1], 128)]
    return (jnp.concatenate(parts, axis=0) * 0.5).astype(BF16)


def masks(tokens):
    row = lax.axis_index("row")
    col = lax.axis_index("col")
    line = tokens[pl.ds(col // 2, 1), :].astype(F32)
    pick = jnp.where(low_lanes((1, 128)), 1, 0) != col % 2
    cols = jnp.where(pick, line, turn(line))
    line = jnp.broadcast_to(tokens[pl.ds(row // 4, 1), :].astype(F32), (32, 128))
    lane = lax.broadcasted_iota(jnp.int32, (32, 128), 1)
    own = lax.broadcasted_iota(jnp.int32, (32, 128), 0) + 32 * (row % 4)
    rows = jnp.sum(jnp.where(lane == own, line, 0.0), axis=1, keepdims=True) * cols
    low = low_lanes((8, 128))
    return jnp.concatenate([jnp.where(low, rows[k : k + 8], rows[k + 8 : k + 16]) for k in (0, 16)], axis=0)


def mask_of(mask, tile):
    return jnp.concatenate([mask[tile : tile + 1], mask[tile + 1 : tile + 2]], axis=1)


def pair_tile(pair, tile):
    place = (tile // 8, slice(None), tile % 8 // 4, tile % 4)
    return pair[place].reshape(128, 128).T


def sides(normed, weights, held, slot):
    linear = dot(weights, normed.astype(BF16))
    left = ((1.0 + jnp.tanh(linear[128:256])) * linear[0:128]).astype(BF16)
    right = ((1.0 + jnp.tanh(linear[384:512])) * linear[256:384]).astype(BF16)
    for k in range(2):
        low = slice(128 * k, 128 * k + HALF)
        high = slice(128 * k + HALF, 128 * (k + 1))
        held[slot + k] = jnp.concatenate([left[:, low], right[:, low]], axis=1)
        held[slot + k + 8] = jnp.concatenate([left[:, high], right[:, high]], axis=1)
    return 1.0 + jnp.tanh(linear[512:640])


def pack(held, out, group):
    for k in range(0, 128, 32):
        out[k : k + 32, 16 * group : 16 * group + 16, :] = jnp.swapaxes(held[:, k : k + 32, :], 0, 1)


def project_kernel(token_h, pair_h, proj_h, out, flat, gating, mask, held, tokens, pair, proj, semaphores):
    parts = [(group, slice(None), part) for group in (0, 1) for part in (0, 1)]
    copies = [
        pltpu.make_async_copy(pair_h.at[part], pair.at[part], semaphores.at[k])
        for k, part in enumerate(parts)
    ]
    weight_copy = pltpu.make_async_copy(proj_h, proj, semaphores.at[4])
    token_copy = pltpu.make_async_copy(token_h, tokens, semaphores.at[5])
    for copy in [weight_copy, token_copy] + copies:
        copy.start()
    for copy in copies:
        copy.wait()
    weight_copy.wait()
    token_copy.wait()
    weights = halved(proj)
    mask[...] = masks(tokens)
    for group in range(2):
        for slot in range(0, 8, 2):
            tile = 8 * group + slot
            lanes = slice(128 * tile, 128 * (tile + 2))
            values = jnp.concatenate([pair_tile(pair, tile), pair_tile(pair, tile + 1)], axis=1)
            flat[:, lanes] = values
            gating[:, lanes] = sides(norm(values, mask_of(mask, tile)), weights, held, slot)
        pack(held, out, group)


def operands(got, left, right):
    for k in range(4):
        lanes = slice(128 * k, 128 * (k + 1))
        even = got[:, 2 * k].reshape(512, 128)
        odd = got[:, 2 * k + 1].reshape(512, 128)
        left[:, lanes] = jnp.concatenate([even[:, :HALF], odd[:, :HALF]], axis=1)
        right[:, lanes] = jnp.concatenate([even[:, HALF:], odd[:, HALF:]], axis=1)


def triangle_kernel(contract, got, out, left, right):
    operands(got, left, right)
    low = low_lanes((16, 128))
    for k in range(0, 16, 16):
        rows = slice(32 * k, 32 * (k + 16))
        if contract == 1:
            sums = dot(left[rows, :], right[...], ((1,), (1,)))
        else:
            sums = dot(left[:, rows], right[...], ((0,), (0,)))
        sums = sums.reshape(16, 2, 2, 8, 512)
        for n in range(16):
            for m in range(4):
                lanes = slice(128 * m, 128 * (m + 1))
                top = sums[n, :, 0, :, lanes].reshape(16, 128)
                bottom = sums[n, :, 1, :, lanes].reshape(16, 128)
                out[k + n, 2 * m] = jnp.where(low, top, turn(bottom)).astype(BF16)
                out[k + n, 2 * m + 1] = jnp.where(low, turn(top), bottom).astype(BF16)


def unpack(got, triangle):
    for k in range(0, 128, 32):
        triangle[:, k : k + 32, :] = jnp.swapaxes(got[k : k + 32], 0, 1)


def finish(triangle, tile, flat, gating, closing):
    lanes = slice(128 * tile, 128 * (tile + 2))
    sums = jnp.concatenate([triangle[tile], triangle[tile + 1]], axis=1).astype(F32)
    return flat[:, lanes] + gating[:, lanes] * dot(closing, norm(sums).astype(BF16))


def middle_kernel(
    mask, got, flat, gating, final, proj, out, first, next_gating, held, triangle
):
    weights = halved(proj)
    closing = halved(final)
    unpack(got, triangle)
    for group in range(2):
        for slot in range(0, 8, 2):
            tile = 8 * group + slot
            lanes = slice(128 * tile, 128 * (tile + 2))
            values = finish(triangle, tile, flat, gating, closing)
            first[:, lanes] = values
            next_gating[:, lanes] = sides(norm(values, mask_of(mask, tile)), weights, held, slot)
        pack(held, out, group)


def last_kernel(got, first, gating, final, out, triangle, done, semaphores):
    closing = halved(final)
    unpack(got, triangle)
    copies = []
    for tile in range(0, TILES, 2):
        values = finish(triangle, tile, first, gating, closing)
        row = (tile // 8) * 16 + tile % 8
        for k in range(2):
            part = values[:, 128 * k : 128 * (k + 1)].T
            done[row + k] = part[:HALF]
            done[row + k + 8] = part[HALF:]
        if tile % 4 == 2:
            for start in (row - 2, row + 6):
                copies.append(
                    pltpu.make_async_copy(
                        done.at[pl.ds(start, 4)], out.at[pl.ds(start, 4)], semaphores.at[len(copies)]
                    )
                )
                copies[-1].start()
    for copy in copies:
        copy.wait()


def shards(pair, token_mask, out_proj, out_final, in_proj, in_final):
    axes = ("row", "col")
    struct = jax.ShapeDtypeStruct
    lines = token_mask.reshape(4, 128)
    message = struct((128, 32, 128), BF16)
    answer = struct((16, 8, 16, 128), BF16)
    whole = struct((128, 2048), F32)
    held = pltpu.VMEM((16, 128, 128), BF16)
    operand = pltpu.VMEM((512, 512), BF16)

    def swap(values):
        return lax.all_to_all(values, axes, 0, 0, tiled=True)

    def triangle(got, contract):
        kernel = functools.partial(triangle_kernel, contract)
        sums = call(kernel, answer, [operand, operand], [VMEM], 2 * 512**3)(got.reshape(16, 8, 32, 128))
        return sums.reshape(128, 16, 128)

    scratch = [
        held,
        pltpu.VMEM((4, 128), jnp.int32),
        pltpu.VMEM((2, 2, 2, 4, 64, 128), F32),
        pltpu.VMEM(out_proj.shape, F32),
        pltpu.SemaphoreType.DMA((6,)),
    ]
    sent, flat, gating, mask = call(
        project_kernel, (message, whole, whole, struct((TILES, 128), F32)), scratch, [HBM] * 3, 2 * 2048 * 128 * 640
    )(*[pltpu.with_memory_space_constraint(v, pltpu.HBM) for v in (lines, pair.reshape(2, 2, 2, 4, 64, 128), out_proj)])
    sums = swap(triangle(swap(sent), 1))
    sent, first, gating = call(
        middle_kernel, (message, whole, whole), [held, held], [VMEM] * 6, 2 * 2048 * 128 * 768
    )(mask, sums, flat, gating, out_final, in_proj)
    sums = swap(triangle(swap(sent), 0))
    return pl.pallas_call(
        last_kernel,
        out_shape=struct(pair.shape, F32),
        in_specs=[VMEM] * 4,
        out_specs=HBM,
        scratch_shapes=[held, pltpu.VMEM(pair.shape, F32), pltpu.SemaphoreType.DMA((8,))],
        compiler_params=pltpu.CompilerParams(vmem_limit_bytes=16 * 1024 * 1024),
        cost_estimate=pl.CostEstimate(flops=2 * 2048 * 128 * 128, bytes_accessed=3 << 20, transcendentals=0),
    )(sums, first, gating, in_final)


def solution(mesh):
    placed = (P("row", "col", None), P(), P(), P(), P(), P())
    return jax.shard_map(
        shards, mesh=mesh, in_specs=placed, out_specs=P("row", "col", None), check_vma=False
    )
```

```python
import functools

import jax
import jax.numpy as jnp
from jax import lax
from jax.experimental import pallas as pl
from jax.experimental.pallas import tpu as pltpu
from jax.sharding import PartitionSpec as P

HALF = 64
TILES = 16
F32 = jnp.float32
BF16 = jnp.bfloat16
VMEM = pl.BlockSpec(memory_space=pltpu.VMEM)
SMEM = pl.BlockSpec(memory_space=pltpu.SMEM)
HBM = pl.BlockSpec(memory_space=pltpu.HBM)


def call(kernel, outs, scratch, specs, flops, limit=16):
    return pl.pallas_call(
        kernel,
        out_shape=outs,
        in_specs=specs,
        out_specs=jax.tree.map(lambda _: VMEM, outs),
        scratch_shapes=scratch,
        compiler_params=pltpu.CompilerParams(vmem_limit_bytes=limit * 1024 * 1024),
        cost_estimate=pl.CostEstimate(flops=flops, bytes_accessed=3 << 20, transcendentals=1 << 19),
    )


def low_lanes(shape):
    return lax.broadcasted_iota(jnp.int32, shape, len(shape) - 1) < HALF


def turn(values):
    return pltpu.roll(values, HALF, axis=values.ndim - 1)


def norm(values, mask=None):
    scale = 1.0 / values.shape[0]
    centred = values - jnp.sum(values, axis=0, keepdims=True) * scale
    factor = lax.rsqrt(jnp.sum(centred * centred, axis=0, keepdims=True) * scale + 1e-05)
    return centred * (factor if mask is None else factor * mask)


def dot(left, right, dims=((1,), (0,))):
    return lax.dot_general(left, right, (dims, ((), ())), preferred_element_type=F32)


def halved(weights):
    parts = [weights[:, k : k + 128].T for k in range(0, weights.shape[1], 128)]
    return (jnp.concatenate(parts, axis=0) * 0.5).astype(BF16)


def masks(tokens):
    row = lax.axis_index("row")
    col = lax.axis_index("col")
    line = tokens[pl.ds(col // 2, 1), :].astype(F32)
    pick = jnp.where(low_lanes((1, 128)), 1, 0) != col % 2
    cols = jnp.where(pick, line, turn(line))
    line = jnp.broadcast_to(tokens[pl.ds(row // 4, 1), :].astype(F32), (32, 128))
    lane = lax.broadcasted_iota(jnp.int32, (32, 128), 1)
    own = lax.broadcasted_iota(jnp.int32, (32, 128), 0) + 32 * (row % 4)
    rows = jnp.sum(jnp.where(lane == own, line, 0.0), axis=1, keepdims=True) * cols
    low = low_lanes((8, 128))
    return jnp.concatenate([jnp.where(low, rows[k : k + 8], rows[k + 8 : k + 16]) for k in (0, 16)], axis=0)


def mask_of(mask, tile):
    return jnp.concatenate([mask[tile : tile + 1], mask[tile + 1 : tile + 2]], axis=1)


def pair_tile(pair, tile):
    place = (tile // 8, slice(None), tile % 8 // 4, tile % 4)
    return pair[place].reshape(128, 128).T


def sides(normed, weights, held, slot):
    linear = dot(weights, normed.astype(BF16))
    left = ((1.0 + jnp.tanh(linear[128:256])) * linear[0:128]).astype(BF16)
    right = ((1.0 + jnp.tanh(linear[384:512])) * linear[256:384]).astype(BF16)
    for k in range(2):
        low = slice(128 * k, 128 * k + HALF)
        high = slice(128 * k + HALF, 128 * (k + 1))
        held[slot + k] = jnp.concatenate([left[:, low], right[:, low]], axis=1)
        held[slot + k + 8] = jnp.concatenate([left[:, high], right[:, high]], axis=1)
    return 1.0 + jnp.tanh(linear[512:640])


def pack(held, out, group):
    for k in range(0, 128, 32):
        out[k : k + 32, 16 * group : 16 * group + 16, :] = jnp.swapaxes(held[:, k : k + 32, :], 0, 1)


def project_kernel(token_h, pair_h, proj_h, out, flat, gating, mask, held, tokens, pair, proj, semaphores):
    parts = [(group, slice(None), part) for group in (0, 1) for part in (0, 1)]
    copies = [
        pltpu.make_async_copy(pair_h.at[part], pair.at[part], semaphores.at[k])
        for k, part in enumerate(parts)
    ]
    weight_copy = pltpu.make_async_copy(proj_h, proj, semaphores.at[4])
    token_copy = pltpu.make_async_copy(token_h, tokens, semaphores.at[5])
    for copy in [weight_copy, token_copy] + copies:
        copy.start()
    for copy in copies:
        copy.wait()
    weight_copy.wait()
    token_copy.wait()
    weights = halved(proj)
    mask[...] = masks(tokens)
    for group in range(2):
        for slot in range(0, 8, 2):
            tile = 8 * group + slot
            lanes = slice(128 * tile, 128 * (tile + 2))
            values = jnp.concatenate([pair_tile(pair, tile), pair_tile(pair, tile + 1)], axis=1)
            flat[:, lanes] = values
            gating[:, lanes] = sides(norm(values, mask_of(mask, tile)), weights, held, slot)
        pack(held, out, group)


def operands(got, left, right):
    for k in range(4):
        lanes = slice(128 * k, 128 * (k + 1))
        even = got[:, 2 * k].reshape(512, 128)
        odd = got[:, 2 * k + 1].reshape(512, 128)
        left[:, lanes] = jnp.concatenate([even[:, :HALF], odd[:, :HALF]], axis=1)
        right[:, lanes] = jnp.concatenate([even[:, HALF:], odd[:, HALF:]], axis=1)


def triangle_kernel(contract, got, out, left, right):
    operands(got, left, right)
    low = low_lanes((16, 128))
    for k in range(0, 16, 16):
        rows = slice(32 * k, 32 * (k + 16))
        if contract == 1:
            sums = dot(left[rows, :], right[...], ((1,), (1,)))
        else:
            sums = dot(left[:, rows], right[...], ((0,), (0,)))
        sums = sums.reshape(16, 2, 2, 8, 512)
        for n in range(16):
            for m in range(4):
                lanes = slice(128 * m, 128 * (m + 1))
                top = sums[n, :, 0, :, lanes].reshape(16, 128)
                bottom = sums[n, :, 1, :, lanes].reshape(16, 128)
                out[k + n, 2 * m] = jnp.where(low, top, turn(bottom)).astype(BF16)
                out[k + n, 2 * m + 1] = jnp.where(low, turn(top), bottom).astype(BF16)


def unpack(got, triangle):
    for k in range(0, 128, 32):
        triangle[:, k : k + 32, :] = jnp.swapaxes(got[k : k + 32], 0, 1)


def finish(triangle, tile, flat, gating, closing):
    lanes = slice(128 * tile, 128 * (tile + 2))
    sums = jnp.concatenate([triangle[tile], triangle[tile + 1]], axis=1).astype(F32)
    return flat[:, lanes] + gating[:, lanes] * dot(closing, norm(sums).astype(BF16))


def middle_kernel(
    mask, got, flat, gating, final, proj, out, first, next_gating, held, triangle
):
    weights = halved(proj)
    closing = halved(final)
    unpack(got, triangle)
    for tile in range(0, TILES, 2):
        first[:, 128 * tile : 128 * (tile + 2)] = finish(triangle, tile, flat, gating, closing)
    for group in range(2):
        for slot in range(0, 8, 2):
            tile = 8 * group + slot
            lanes = slice(128 * tile, 128 * (tile + 2))
            next_gating[:, lanes] = sides(norm(first[:, lanes], mask_of(mask, tile)), weights, held, slot)
        pack(held, out, group)


def last_kernel(got, first, gating, final, out, triangle, done, semaphores):
    closing = halved(final)
    unpack(got, triangle)
    copies = []
    for tile in range(0, TILES, 2):
        values = finish(triangle, tile, first, gating, closing)
        row = (tile // 8) * 16 + tile % 8
        for k in range(2):
            part = values[:, 128 * k : 128 * (k + 1)].T
            done[row + k] = part[:HALF]
            done[row + k + 8] = part[HALF:]
        if tile % 4 == 2:
            for start in (row - 2, row + 6):
                copies.append(
                    pltpu.make_async_copy(
                        done.at[pl.ds(start, 4)], out.at[pl.ds(start, 4)], semaphores.at[len(copies)]
                    )
                )
                copies[-1].start()
    for copy in copies:
        copy.wait()


def shards(pair, token_mask, out_proj, out_final, in_proj, in_final):
    axes = ("row", "col")
    struct = jax.ShapeDtypeStruct
    lines = token_mask.reshape(4, 128)
    message = struct((128, 32, 128), BF16)
    answer = struct((16, 8, 16, 128), BF16)
    whole = struct((128, 2048), F32)
    held = pltpu.VMEM((16, 128, 128), BF16)
    operand = pltpu.VMEM((512, 512), BF16)

    def swap(values):
        return lax.all_to_all(values, axes, 0, 0, tiled=True)

    def triangle(got, contract):
        kernel = functools.partial(triangle_kernel, contract)
        sums = call(kernel, answer, [operand, operand], [VMEM], 2 * 512**3)(got.reshape(16, 8, 32, 128))
        return sums.reshape(128, 16, 128)

    scratch = [
        held,
        pltpu.VMEM((4, 128), jnp.int32),
        pltpu.VMEM((2, 2, 2, 4, 64, 128), F32),
        pltpu.VMEM(out_proj.shape, F32),
        pltpu.SemaphoreType.DMA((6,)),
    ]
    sent, flat, gating, mask = call(
        project_kernel, (message, whole, whole, struct((TILES, 128), F32)), scratch, [HBM] * 3, 2 * 2048 * 128 * 640
    )(*[pltpu.with_memory_space_constraint(v, pltpu.HBM) for v in (lines, pair.reshape(2, 2, 2, 4, 64, 128), out_proj)])
    sums = swap(triangle(swap(sent), 1))
    sent, first, gating = call(
        middle_kernel, (message, whole, whole), [held, held], [VMEM] * 6, 2 * 2048 * 128 * 768
    )(mask, sums, flat, gating, out_final, in_proj)
    sums = swap(triangle(swap(sent), 0))
    return pl.pallas_call(
        last_kernel,
        out_shape=struct(pair.shape, F32),
        in_specs=[VMEM] * 4,
        out_specs=HBM,
        scratch_shapes=[held, pltpu.VMEM(pair.shape, F32), pltpu.SemaphoreType.DMA((8,))],
        compiler_params=pltpu.CompilerParams(vmem_limit_bytes=16 * 1024 * 1024),
        cost_estimate=pl.CostEstimate(flops=2 * 2048 * 128 * 128, bytes_accessed=3 << 20, transcendentals=0),
    )(sums, first, gating, in_final)


def solution(mesh):
    placed = (P("row", "col", None), P(), P(), P(), P(), P())
    return jax.shard_map(
        shards, mesh=mesh, in_specs=placed, out_specs=P("row", "col", None), check_vma=False
    )
```

```python
import functools

import jax
import jax.numpy as jnp
from jax import lax
from jax.experimental import pallas as pl
from jax.experimental.pallas import tpu as pltpu
from jax.sharding import PartitionSpec as P

HALF = 64
TILES = 16
F32 = jnp.float32
BF16 = jnp.bfloat16
VMEM = pl.BlockSpec(memory_space=pltpu.VMEM)
SMEM = pl.BlockSpec(memory_space=pltpu.SMEM)
HBM = pl.BlockSpec(memory_space=pltpu.HBM)


def call(kernel, outs, scratch, specs, flops, limit=16):
    return pl.pallas_call(
        kernel,
        out_shape=outs,
        in_specs=specs,
        out_specs=jax.tree.map(lambda _: VMEM, outs),
        scratch_shapes=scratch,
        compiler_params=pltpu.CompilerParams(vmem_limit_bytes=limit * 1024 * 1024),
        cost_estimate=pl.CostEstimate(flops=flops, bytes_accessed=3 << 20, transcendentals=1 << 19),
    )


def low_lanes(shape):
    return lax.broadcasted_iota(jnp.int32, shape, len(shape) - 1) < HALF


def turn(values):
    return pltpu.roll(values, HALF, axis=values.ndim - 1)


def norm(values, mask=None):
    scale = 1.0 / values.shape[0]
    centred = values - jnp.sum(values, axis=0, keepdims=True) * scale
    factor = lax.rsqrt(jnp.sum(centred * centred, axis=0, keepdims=True) * scale + 1e-05)
    return centred * (factor if mask is None else factor * mask)


def dot(left, right, dims=((1,), (0,))):
    return lax.dot_general(left, right, (dims, ((), ())), preferred_element_type=F32)


def split(values):
    high = values.astype(BF16)
    return high, (values - high.astype(F32)).astype(BF16)


def halved(weights):
    order = (0, 256, 128, 384, 512) if weights.shape[1] == 640 else (0,)
    parts = [weights[:, k : k + 128].T for k in order]
    high, low = split(jnp.concatenate(parts, axis=0) * 0.5)
    return jnp.concatenate([high, high, low], axis=1)


def masks(tokens):
    row = lax.axis_index("row")
    col = lax.axis_index("col")
    line = tokens[pl.ds(col // 2, 1), :].astype(F32)
    pick = jnp.where(low_lanes((1, 128)), 1, 0) != col % 2
    cols = jnp.where(pick, line, turn(line))
    line = jnp.broadcast_to(tokens[pl.ds(row // 4, 1), :].astype(F32), (32, 128))
    lane = lax.broadcasted_iota(jnp.int32, (32, 128), 1)
    own = lax.broadcasted_iota(jnp.int32, (32, 128), 0) + 32 * (row % 4)
    rows = jnp.sum(jnp.where(lane == own, line, 0.0), axis=1, keepdims=True) * cols
    return jnp.where(low_lanes((TILES, 128)), rows[:TILES], rows[TILES:])


def mask_of(mask, tile):
    return jnp.concatenate([mask[tile : tile + 1], mask[tile + 1 : tile + 2]], axis=1)


def pair_tile(pair, tile):
    return pair[:, tile].reshape(128, 128).T


def three(weights, values):
    high, low = split(values)
    return dot(weights, jnp.concatenate([high, low, high], axis=0))


def sides(normed, weights, held, tile):
    high, low = split(normed)
    both = jnp.concatenate([high, low], axis=0)
    gates = dot(weights[256:, :256], both)
    sided = dot(weights[:256, :256], both) + dot(weights[:256, 256:], high)
    left = ((1.0 + jnp.tanh(gates[:128])) * sided[:128]).astype(BF16)
    right = ((1.0 + jnp.tanh(gates[128:256])) * sided[128:]).astype(BF16)
    for k in range(2):
        lanes = slice(128 * k, 128 * (k + 1))
        held[0, tile + k] = left[:, lanes]
        held[1, tile + k] = right[:, lanes]
    return 1.0 + jnp.tanh(gates[256:])


def pack(held, out):
    for side in range(2):
        for k in range(0, 128, 32):
            out[k : k + 32, 16 * side : 16 * side + 16, :] = jnp.swapaxes(held[side, :, k : k + 32, :], 0, 1)


def project_kernel(token_h, pair_h, proj_h, out, flat, gating, mask, held, tokens, pair, proj, semaphores):
    parts = [(slice(None), pl.ds(4 * k, 4)) for k in range(4)]
    copies = [
        pltpu.make_async_copy(pair_h.at[part], pair.at[part], semaphores.at[k])
        for k, part in enumerate(parts)
    ]
    weight_copy = pltpu.make_async_copy(proj_h, proj, semaphores.at[4])
    token_copy = pltpu.make_async_copy(token_h, tokens, semaphores.at[5])
    for copy in [weight_copy, token_copy] + copies:
        copy.start()
    for copy in copies:
        copy.wait()
    weight_copy.wait()
    token_copy.wait()
    weights = halved(proj)
    mask[...] = masks(tokens)
    for tile in range(0, TILES, 2):
        lanes = slice(128 * tile, 128 * (tile + 2))
        values = jnp.concatenate([pair_tile(pair, tile), pair_tile(pair, tile + 1)], axis=1)
        flat[:, lanes] = values
        gating[:, lanes] = sides(norm(values, mask_of(mask, tile)), weights, held, tile)
    pack(held, out)


def operands(got, left, right):
    for side, matrix in enumerate((left, right)):
        for k in range(4):
            lanes = slice(128 * k, 128 * (k + 1))
            even = got[:, 2 * k, 16 * side : 16 * side + 16]
            odd = got[:, 2 * k + 1, 16 * side : 16 * side + 16]
            matrix[:, 0, :, lanes] = jnp.concatenate([even[..., :HALF], odd[..., :HALF]], axis=2)
            matrix[:, 1, :, lanes] = jnp.concatenate([even[..., HALF:], odd[..., HALF:]], axis=2)
    return left[...].reshape(512, 512), right[...].reshape(512, 512)


def triangle_kernel(contract, got, out, left, right):
    left, right = operands(got, left, right)
    sums = dot(left, right, ((contract,), (contract,))).reshape(16, 2, 16, 512)
    low = low_lanes((16, 128))
    for n in range(16):
        for m in range(4):
            lanes = slice(128 * m, 128 * (m + 1))
            top, bottom = sums[n, 0, :, lanes], sums[n, 1, :, lanes]
            out[n, 2 * m] = jnp.where(low, top, turn(bottom)).astype(BF16)
            out[n, 2 * m + 1] = jnp.where(low, turn(top), bottom).astype(BF16)


def unpack(got, triangle):
    for k in range(0, 128, 32):
        triangle[:, k : k + 32, :] = jnp.swapaxes(got[k : k + 32], 0, 1)


def finish(triangle, tile, flat, gating, closing):
    lanes = slice(128 * tile, 128 * (tile + 2))
    sums = jnp.concatenate([triangle[tile], triangle[tile + 1]], axis=1).astype(F32)
    return flat[:, lanes] + gating[:, lanes] * three(closing, norm(sums))


def middle_kernel(
    mask, got, flat, gating, final, proj, out, first, next_gating, held, triangle
):
    weights = halved(proj)
    closing = halved(final)
    unpack(got, triangle)
    for tile in range(0, TILES, 2):
        first[:, 128 * tile : 128 * (tile + 2)] = finish(triangle, tile, flat, gating, closing)
    for tile in range(0, TILES, 2):
        lanes = slice(128 * tile, 128 * (tile + 2))
        next_gating[:, lanes] = sides(norm(first[:, lanes], mask_of(mask, tile)), weights, held, tile)
    pack(held, out)


def last_kernel(got, first, gating, final, out, triangle, done, semaphores):
    closing = halved(final)
    unpack(got, triangle)
    copies = []
    for tile in range(0, TILES, 2):
        values = finish(triangle, tile, first, gating, closing)
        for k in range(2):
            part = values[:, 128 * k : 128 * (k + 1)].T
            done[tile + k] = part[:HALF]
            done[tile + k + 16] = part[HALF:]
        if tile % 4 == 2:
            for start in (tile - 2, tile + 14):
                rows = pl.ds(start, 4)
                copies.append(pltpu.make_async_copy(done.at[rows], out.at[rows], semaphores.at[len(copies)]))
                copies[-1].start()
    for copy in copies:
        copy.wait()


def shards(pair, token_mask, out_proj, out_final, in_proj, in_final):
    axes = ("row", "col")
    struct = jax.ShapeDtypeStruct
    lines = token_mask.reshape(4, 128)
    message = struct((128, 32, 128), BF16)
    answer = struct((16, 8, 16, 128), BF16)
    whole = struct((128, 2048), F32)
    held = pltpu.VMEM((2, TILES, 128, 128), BF16)
    sums_held = pltpu.VMEM((TILES, 128, 128), BF16)
    operand = pltpu.VMEM((16, 2, 16, 512), BF16)

    def swap(values):
        return lax.all_to_all(values, axes, 0, 0, tiled=True)

    def triangle(got, contract):
        kernel = functools.partial(triangle_kernel, contract)
        sums = call(kernel, answer, [operand, operand], [VMEM], 2 * 512**3)(got.reshape(16, 8, 32, 128))
        return sums.reshape(128, 16, 128)

    scratch = [
        held,
        pltpu.VMEM((4, 128), jnp.int32),
        pltpu.VMEM((2, TILES, HALF, 128), F32),
        pltpu.VMEM(out_proj.shape, F32),
        pltpu.SemaphoreType.DMA((6,)),
    ]
    sent, flat, gating, mask = call(
        project_kernel, (message, whole, whole, struct((TILES, 128), F32)), scratch, [HBM] * 3, 2 * 2048 * 128 * 640
    )(*[pltpu.with_memory_space_constraint(v, pltpu.HBM) for v in (lines, pair.reshape(2, TILES, HALF, 128), out_proj)])
    sums = swap(triangle(swap(sent), 1))
    sent, first, gating = call(
        middle_kernel, (message, whole, whole), [held, sums_held], [VMEM] * 6, 2 * 2048 * 128 * 768
    )(mask, sums, flat, gating, out_final, in_proj)
    sums = swap(triangle(swap(sent), 0))
    return pl.pallas_call(
        last_kernel,
        out_shape=struct(pair.shape, F32),
        in_specs=[VMEM] * 4,
        out_specs=HBM,
        scratch_shapes=[sums_held, pltpu.VMEM(pair.shape, F32), pltpu.SemaphoreType.DMA((8,))],
        compiler_params=pltpu.CompilerParams(vmem_limit_bytes=16 * 1024 * 1024),
        cost_estimate=pl.CostEstimate(flops=2 * 2048 * 128 * 128, bytes_accessed=3 << 20, transcendentals=0),
    )(sums, first, gating, in_final)


def solution(mesh):
    placed = (P("row", "col", None), P(), P(), P(), P(), P())
    return jax.shard_map(
        shards, mesh=mesh, in_specs=placed, out_specs=P("row", "col", None), check_vma=False
    )
```

```python
import functools

import jax
import jax.numpy as jnp
from jax import lax
from jax.experimental import pallas as pl
from jax.experimental.pallas import tpu as pltpu
from jax.sharding import PartitionSpec as P

HALF = 64
TILES = 16
F32 = jnp.float32
BF16 = jnp.bfloat16
VMEM = pl.BlockSpec(memory_space=pltpu.VMEM)
SMEM = pl.BlockSpec(memory_space=pltpu.SMEM)
HBM = pl.BlockSpec(memory_space=pltpu.HBM)


def call(kernel, outs, scratch, specs, flops, limit=16):
    return pl.pallas_call(
        kernel,
        out_shape=outs,
        in_specs=specs,
        out_specs=jax.tree.map(lambda _: VMEM, outs),
        scratch_shapes=scratch,
        compiler_params=pltpu.CompilerParams(vmem_limit_bytes=limit * 1024 * 1024),
        cost_estimate=pl.CostEstimate(flops=flops, bytes_accessed=3 << 20, transcendentals=1 << 19),
    )


def low_lanes(shape):
    return lax.broadcasted_iota(jnp.int32, shape, len(shape) - 1) < HALF


def turn(values):
    return pltpu.roll(values, HALF, axis=values.ndim - 1)


def norm(values, mask=None):
    scale = 1.0 / values.shape[0]
    centred = values - jnp.sum(values, axis=0, keepdims=True) * scale
    factor = lax.rsqrt(jnp.sum(centred * centred, axis=0, keepdims=True) * scale + 1e-05)
    return centred * (factor if mask is None else factor * mask)


def dot(left, right, dims=((1,), (0,))):
    return lax.dot_general(left, right, (dims, ((), ())), preferred_element_type=F32)


def split(values):
    high = values.astype(BF16)
    return high, (values - high.astype(F32)).astype(BF16)


def halved(weights):
    rows = []
    for k in range(0, weights.shape[1], 128):
        high, low = split(weights[:, k : k + 128].T * 0.5)
        rows.append([jnp.concatenate([high, high], axis=1), jnp.concatenate([low, jnp.zeros_like(low)], axis=1)])
    if len(rows) == 1:
        return jnp.concatenate(rows[0], axis=0)
    return jnp.concatenate(rows[0] + rows[1][:1] + rows[2] + rows[3][:1] + rows[4][:1], axis=0)


def masks(tokens):
    row = lax.axis_index("row")
    col = lax.axis_index("col")
    line = tokens[pl.ds(col // 2, 1), :].astype(F32)
    pick = jnp.where(low_lanes((1, 128)), 1, 0) != col % 2
    cols = jnp.where(pick, line, turn(line))
    line = jnp.broadcast_to(tokens[pl.ds(row // 4, 1), :].astype(F32), (32, 128))
    lane = lax.broadcasted_iota(jnp.int32, (32, 128), 1)
    own = lax.broadcasted_iota(jnp.int32, (32, 128), 0) + 32 * (row % 4)
    rows = jnp.sum(jnp.where(lane == own, line, 0.0), axis=1, keepdims=True) * cols
    return jnp.where(low_lanes((TILES, 128)), rows[:TILES], rows[TILES:])


def mask_of(mask, tile):
    return jnp.concatenate([mask[tile : tile + 1], mask[tile + 1 : tile + 2]], axis=1)


def pair_tile(pair, tile):
    return pair[:, tile].reshape(128, 128).T


def sides(normed, weights, held, tile):
    both = jnp.concatenate(split(normed), axis=0)

    def side(k):
        linear = dot(weights[384 * k : 384 * (k + 1)], both)
        value = linear[:128] + linear[128:256]
        value = value + jnp.tanh(linear[256:]) * value
        for n in range(2):
            held[k, tile + n] = value[:, 128 * n : 128 * (n + 1)]

    side(0)
    side(1)
    return 1.0 + jnp.tanh(dot(weights[768:], both))


def pack(held, out):
    for side in range(2):
        for k in range(0, 128, 32):
            out[k : k + 32, 16 * side : 16 * side + 16, :] = jnp.swapaxes(held[side, :, k : k + 32, :], 0, 1).astype(BF16)


def project_kernel(token_h, pair_h, proj_h, out, flat, gating, mask, held, normed, tokens, pair, proj, semaphores):
    parts = [(slice(None), pl.ds(4 * k, 4)) for k in range(4)]
    copies = [
        pltpu.make_async_copy(pair_h.at[part], pair.at[part], semaphores.at[k])
        for k, part in enumerate(parts)
    ]
    weight_copy = pltpu.make_async_copy(proj_h, proj, semaphores.at[4])
    token_copy = pltpu.make_async_copy(token_h, tokens, semaphores.at[5])
    for copy in [token_copy] + copies[:2] + [weight_copy] + copies[2:]:
        copy.start()
    token_copy.wait()
    copies[0].wait()
    copies[1].wait()
    mask[...] = masks(tokens)
    for tile in range(0, TILES, 2):
        if tile == 8:
            weight_copy.wait()
            copies[2].wait()
            copies[3].wait()
            weights = halved(proj)
        lanes = slice(128 * tile, 128 * (tile + 2))
        values = jnp.concatenate([pair_tile(pair, tile), pair_tile(pair, tile + 1)], axis=1)
        flat[:, lanes] = values
        normed[:, lanes] = norm(values, mask_of(mask, tile))
    for tile in range(0, TILES, 2):
        lanes = slice(128 * tile, 128 * (tile + 2))
        gating[:, lanes] = sides(normed[:, lanes], weights, held, tile)
    pack(held, out)


def operands(got):
    matrices = []
    for side in range(2):
        halves = []
        for lanes in (slice(0, HALF), slice(HALF, 128)):
            parts = [got[:, k, 16 * side : 16 * side + 16, lanes] for k in range(8)]
            halves.append(jnp.concatenate(parts, axis=2))
        matrices.append(jnp.stack(halves, axis=1).reshape(512, 512))
    return matrices


def triangle_kernel(contract, got, out):
    left, right = operands(got)
    sums = dot(left, right, ((contract,), (contract,))).reshape(16, 2, 16, 512)
    low = low_lanes((16, 128))
    for n in range(16):
        for m in range(4):
            lanes = slice(128 * m, 128 * (m + 1))
            top, bottom = sums[n, 0, :, lanes], sums[n, 1, :, lanes]
            out[n, 2 * m] = jnp.where(low, top, turn(bottom)).astype(BF16)
            out[n, 2 * m + 1] = jnp.where(low, turn(top), bottom).astype(BF16)


def unpack(got, triangle):
    for k in range(0, 128, 32):
        triangle[:, k : k + 32, :] = jnp.swapaxes(got[k : k + 32], 0, 1)


def finish(triangle, tile, flat, gating, closing):
    lanes = slice(128 * tile, 128 * (tile + 2))
    sums = jnp.concatenate([triangle[tile], triangle[tile + 1]], axis=1).astype(F32)
    product = dot(closing, jnp.concatenate(split(norm(sums)), axis=0))
    product = product[:128] + product[128:]
    return flat[:, lanes] + gating[:, lanes] * product


def middle_kernel(
    mask, got, flat, gating, final, proj, out, first, next_gating, held, triangle
):
    weights = halved(proj)
    closing = halved(final)
    unpack(got, triangle)
    for tile in range(0, TILES, 2):
        first[:, 128 * tile : 128 * (tile + 2)] = finish(triangle, tile, flat, gating, closing)
    for tile in range(0, TILES, 2):
        lanes = slice(128 * tile, 128 * (tile + 2))
        next_gating[:, lanes] = sides(norm(first[:, lanes], mask_of(mask, tile)), weights, held, tile)
    pack(held, out)


def last_kernel(got, first, gating, final, out, triangle, done, semaphores):
    closing = halved(final)
    unpack(got, triangle)
    copies = []
    for tile in range(0, TILES, 2):
        values = finish(triangle, tile, first, gating, closing)
        for k in range(2):
            part = values[:, 128 * k : 128 * (k + 1)].T
            done[tile + k] = part[:HALF]
            done[tile + k + 16] = part[HALF:]
        if tile % 4 == 2:
            for start in (tile - 2, tile + 14):
                rows = pl.ds(start, 4)
                copies.append(pltpu.make_async_copy(done.at[rows], out.at[rows], semaphores.at[len(copies)]))
                copies[-1].start()
    for copy in copies:
        copy.wait()


def shards(pair, token_mask, out_proj, out_final, in_proj, in_final):
    axes = ("row", "col")
    struct = jax.ShapeDtypeStruct
    lines = token_mask.reshape(4, 128)
    message = struct((128, 32, 128), BF16)
    answer = struct((16, 8, 16, 128), BF16)
    whole = struct((128, 2048), F32)
    held = pltpu.VMEM((2, TILES, 128, 128), F32)
    sums_held = pltpu.VMEM((TILES, 128, 128), BF16)

    def swap(values):
        return lax.all_to_all(values, axes, 0, 0, tiled=True)

    def triangle(got, contract):
        kernel = functools.partial(triangle_kernel, contract)
        sums = call(kernel, answer, [], [VMEM], 2 * 512**3)(got.reshape(16, 8, 32, 128))
        return sums.reshape(128, 16, 128)

    scratch = [
        held,
        pltpu.VMEM((128, 2048), F32),
        pltpu.VMEM((4, 128), jnp.int32),
        pltpu.VMEM((2, TILES, HALF, 128), F32),
        pltpu.VMEM(out_proj.shape, F32),
        pltpu.SemaphoreType.DMA((6,)),
    ]
    sent, flat, gating, mask = call(
        project_kernel, (message, whole, whole, struct((TILES, 128), F32)), scratch, [HBM] * 3, 2 * 2048 * 128 * 640
    )(*[pltpu.with_memory_space_constraint(v, pltpu.HBM) for v in (lines, pair.reshape(2, TILES, HALF, 128), out_proj)])
    sums = swap(triangle(swap(sent), 1))
    sent, first, gating = call(
        middle_kernel, (message, whole, whole), [held, sums_held], [VMEM] * 6, 2 * 2048 * 128 * 768
    )(mask, sums, flat, gating, out_final, in_proj)
    sums = swap(triangle(swap(sent), 0))
    return pl.pallas_call(
        last_kernel,
        out_shape=struct(pair.shape, F32),
        in_specs=[VMEM] * 4,
        out_specs=HBM,
        scratch_shapes=[sums_held, pltpu.VMEM(pair.shape, F32), pltpu.SemaphoreType.DMA((8,))],
        compiler_params=pltpu.CompilerParams(vmem_limit_bytes=16 * 1024 * 1024),
        cost_estimate=pl.CostEstimate(flops=2 * 2048 * 128 * 128, bytes_accessed=3 << 20, transcendentals=0),
    )(sums, first, gating, in_final)


def solution(mesh):
    placed = (P("row", "col", None), P(), P(), P(), P(), P())
    return jax.shard_map(
        shards, mesh=mesh, in_specs=placed, out_specs=P("row", "col", None), check_vma=False
    )
```

```python
import functools

import jax
import jax.numpy as jnp
from jax import lax
from jax.experimental import pallas as pl
from jax.experimental.pallas import tpu as pltpu
from jax.sharding import PartitionSpec as P

HALF = 64
TILES = 16
F32 = jnp.float32
BF16 = jnp.bfloat16
VMEM = pl.BlockSpec(memory_space=pltpu.VMEM)
SMEM = pl.BlockSpec(memory_space=pltpu.SMEM)
HBM = pl.BlockSpec(memory_space=pltpu.HBM)


def call(kernel, outs, scratch, specs, flops, limit=16):
    return pl.pallas_call(
        kernel,
        out_shape=outs,
        in_specs=specs,
        out_specs=jax.tree.map(lambda _: VMEM, outs),
        scratch_shapes=scratch,
        compiler_params=pltpu.CompilerParams(vmem_limit_bytes=limit * 1024 * 1024),
        cost_estimate=pl.CostEstimate(flops=flops, bytes_accessed=3 << 20, transcendentals=1 << 19),
    )


def low_lanes(shape):
    return lax.broadcasted_iota(jnp.int32, shape, len(shape) - 1) < HALF


def turn(values):
    return pltpu.roll(values, HALF, axis=values.ndim - 1)


def norm(values, mask=None):
    scale = 1.0 / values.shape[0]
    centred = values - jnp.sum(values, axis=0, keepdims=True) * scale
    factor = lax.rsqrt(jnp.sum(centred * centred, axis=0, keepdims=True) * scale + 1e-05)
    return centred * (factor if mask is None else factor * mask)


def dot(left, right, dims=((1,), (0,))):
    return lax.dot_general(left, right, (dims, ((), ())), preferred_element_type=F32)


def split(values):
    high = values.astype(BF16)
    return high, (values - high.astype(F32)).astype(BF16)


def halved(weights):
    rows = []
    for k in range(0, weights.shape[1], 128):
        high, low = split(weights[:, k : k + 128].T * 0.5)
        rows.append([jnp.concatenate([high, high], axis=1), jnp.concatenate([low, jnp.zeros_like(low)], axis=1)])
    if len(rows) == 1:
        return jnp.concatenate(rows[0], axis=0)
    return jnp.concatenate(rows[0] + rows[1][:1] + rows[2] + rows[3][:1] + rows[4][:1], axis=0)


def masks(tokens):
    row = lax.axis_index("row")
    col = lax.axis_index("col")
    line = tokens[pl.ds(col // 2, 1), :].astype(F32)
    pick = jnp.where(low_lanes((1, 128)), 1, 0) != col % 2
    cols = jnp.where(pick, line, turn(line))
    line = jnp.broadcast_to(tokens[pl.ds(row // 4, 1), :].astype(F32), (32, 128))
    lane = lax.broadcasted_iota(jnp.int32, (32, 128), 1)
    own = lax.broadcasted_iota(jnp.int32, (32, 128), 0) + 32 * (row % 4)
    rows = jnp.sum(jnp.where(lane == own, line, 0.0), axis=1, keepdims=True) * cols
    return jnp.where(low_lanes((TILES, 128)), rows[:TILES], rows[TILES:])


def mask_of(mask, tile):
    return jnp.concatenate([mask[tile : tile + 1], mask[tile + 1 : tile + 2]], axis=1)


def pair_tile(pair, tile):
    return pair[:, tile].reshape(128, 128).T


def sides(normed, weights, held, tile):
    both = jnp.concatenate(split(normed), axis=0)

    def side(k):
        linear = dot(weights[384 * k : 384 * (k + 1)], both)
        value = linear[:128] + linear[128:256]
        value = value + jnp.tanh(linear[256:]) * value
        for n in range(2):
            held[k, tile + n] = value[:, 128 * n : 128 * (n + 1)]

    side(0)
    side(1)
    return 1.0 + jnp.tanh(dot(weights[768:], both))


def pack(held, out):
    for side in range(2):
        for k in range(0, 128, 32):
            out[k : k + 32, 16 * side : 16 * side + 16, :] = jnp.swapaxes(held[side, :, k : k + 32, :], 0, 1).astype(BF16)


def project_kernel(token_h, pair_h, proj_h, out, flat, gating, mask, held, normed, tokens, pair, proj, semaphores):
    parts = [(slice(None), pl.ds(4 * k, 4)) for k in range(4)]
    copies = [
        pltpu.make_async_copy(pair_h.at[part], pair.at[part], semaphores.at[k])
        for k, part in enumerate(parts)
    ]
    weight_copy = pltpu.make_async_copy(proj_h, proj, semaphores.at[4])
    token_copy = pltpu.make_async_copy(token_h, tokens, semaphores.at[5])
    for copy in [token_copy] + copies[:2] + [weight_copy] + copies[2:]:
        copy.start()
    token_copy.wait()
    copies[0].wait()
    copies[1].wait()
    mask[...] = masks(tokens)
    for tile in range(0, TILES, 2):
        if tile == 8:
            weight_copy.wait()
            copies[2].wait()
            copies[3].wait()
            weights = halved(proj)
        lanes = slice(128 * tile, 128 * (tile + 2))
        values = jnp.concatenate([pair_tile(pair, tile), pair_tile(pair, tile + 1)], axis=1)
        flat[:, lanes] = values
        normed[:, lanes] = norm(values, mask_of(mask, tile))
    for tile in range(0, TILES, 2):
        lanes = slice(128 * tile, 128 * (tile + 2))
        gating[:, lanes] = sides(normed[:, lanes], weights, held, tile)
    pack(held, out)


def operands(got):
    matrices = []
    for side in range(2):
        halves = []
        for lanes in (slice(0, HALF), slice(HALF, 128)):
            parts = [got[:, k, 16 * side : 16 * side + 16, lanes] for k in range(8)]
            halves.append(jnp.concatenate(parts, axis=2))
        matrices.append(jnp.stack(halves, axis=1).reshape(512, 512))
    return matrices


def triangle_kernel(contract, got, out):
    left, right = operands(got)
    sums = dot(left, right, ((contract,), (contract,))).reshape(16, 2, 16, 512)
    low = low_lanes((16, 128))
    for n in range(16):
        for m in range(4):
            lanes = slice(128 * m, 128 * (m + 1))
            top, bottom = sums[n, 0, :, lanes], sums[n, 1, :, lanes]
            out[n, 2 * m] = jnp.where(low, top, turn(bottom)).astype(BF16)
            out[n, 2 * m + 1] = jnp.where(low, turn(top), bottom).astype(BF16)


def unpack(got):
    return jnp.swapaxes(got[...], 0, 1)


def finish(triangle, tile, flat, gating, closing):
    lanes = slice(128 * tile, 128 * (tile + 2))
    sums = jnp.concatenate([triangle[tile], triangle[tile + 1]], axis=1).astype(F32)
    product = dot(closing, jnp.concatenate(split(norm(sums)), axis=0))
    product = product[:128] + product[128:]
    return flat[:, lanes] + gating[:, lanes] * product


def middle_kernel(
    mask, got, flat, gating, final, proj, out, first, next_gating, held
):
    weights = halved(proj)
    closing = halved(final)
    triangle = unpack(got)
    for tile in range(0, TILES, 2):
        first[:, 128 * tile : 128 * (tile + 2)] = finish(triangle, tile, flat, gating, closing)
    for tile in range(0, TILES, 2):
        lanes = slice(128 * tile, 128 * (tile + 2))
        next_gating[:, lanes] = sides(norm(first[:, lanes], mask_of(mask, tile)), weights, held, tile)
    pack(held, out)


def last_kernel(got, first, gating, final, out, done, semaphores):
    closing = halved(final)
    triangle = unpack(got)
    copies = []
    for tile in range(0, TILES, 2):
        values = finish(triangle, tile, first, gating, closing)
        for k in range(2):
            part = values[:, 128 * k : 128 * (k + 1)].T
            done[tile + k] = part[:HALF]
            done[tile + k + 16] = part[HALF:]
        if tile % 4 == 2:
            for start in (tile - 2, tile + 14):
                rows = pl.ds(start, 4)
                copies.append(pltpu.make_async_copy(done.at[rows], out.at[rows], semaphores.at[len(copies)]))
                copies[-1].start()
    for copy in copies:
        copy.wait()


def shards(pair, token_mask, out_proj, out_final, in_proj, in_final):
    axes = ("row", "col")
    struct = jax.ShapeDtypeStruct
    lines = token_mask.reshape(4, 128)
    message = struct((128, 32, 128), BF16)
    answer = struct((16, 8, 16, 128), BF16)
    whole = struct((128, 2048), F32)
    held = pltpu.VMEM((2, TILES, 128, 128), F32)

    def swap(values):
        return lax.all_to_all(values, axes, 0, 0, tiled=True)

    def triangle(got, contract):
        kernel = functools.partial(triangle_kernel, contract)
        sums = call(kernel, answer, [], [VMEM], 2 * 512**3)(got.reshape(16, 8, 32, 128))
        return sums.reshape(128, 16, 128)

    scratch = [
        held,
        pltpu.VMEM((128, 2048), F32),
        pltpu.VMEM((4, 128), jnp.int32),
        pltpu.VMEM((2, TILES, HALF, 128), F32),
        pltpu.VMEM(out_proj.shape, F32),
        pltpu.SemaphoreType.DMA((6,)),
    ]
    sent, flat, gating, mask = call(
        project_kernel, (message, whole, whole, struct((TILES, 128), F32)), scratch, [HBM] * 3, 2 * 2048 * 128 * 640
    )(*[pltpu.with_memory_space_constraint(v, pltpu.HBM) for v in (lines, pair.reshape(2, TILES, HALF, 128), out_proj)])
    sums = swap(triangle(swap(sent), 1))
    sent, first, gating = call(
        middle_kernel, (message, whole, whole), [held], [VMEM] * 6, 2 * 2048 * 128 * 768
    )(mask, sums, flat, gating, out_final, in_proj)
    sums = swap(triangle(swap(sent), 0))
    return pl.pallas_call(
        last_kernel,
        out_shape=struct(pair.shape, F32),
        in_specs=[VMEM] * 4,
        out_specs=HBM,
        scratch_shapes=[pltpu.VMEM(pair.shape, F32), pltpu.SemaphoreType.DMA((8,))],
        compiler_params=pltpu.CompilerParams(vmem_limit_bytes=16 * 1024 * 1024),
        cost_estimate=pl.CostEstimate(flops=2 * 2048 * 128 * 128, bytes_accessed=3 << 20, transcendentals=0),
    )(sums, first, gating, in_final)


def solution(mesh):
    placed = (P("row", "col", None), P(), P(), P(), P(), P())
    return jax.shard_map(
        shards, mesh=mesh, in_specs=placed, out_specs=P("row", "col", None), check_vma=False
    )
```

```python
import functools

import jax
import jax.numpy as jnp
from jax import lax
from jax.experimental import pallas as pl
from jax.experimental.pallas import tpu as pltpu
from jax.sharding import PartitionSpec as P

HALF = 64
TILES = 16
F32 = jnp.float32
BF16 = jnp.bfloat16
VMEM = pl.BlockSpec(memory_space=pltpu.VMEM)
SMEM = pl.BlockSpec(memory_space=pltpu.SMEM)
HBM = pl.BlockSpec(memory_space=pltpu.HBM)


def call(kernel, outs, scratch, specs, flops, limit=16):
    return pl.pallas_call(
        kernel,
        out_shape=outs,
        in_specs=specs,
        out_specs=jax.tree.map(lambda _: VMEM, outs),
        scratch_shapes=scratch,
        compiler_params=pltpu.CompilerParams(vmem_limit_bytes=limit * 1024 * 1024),
        cost_estimate=pl.CostEstimate(flops=flops, bytes_accessed=3 << 20, transcendentals=1 << 19),
    )


def low_lanes(shape):
    return lax.broadcasted_iota(jnp.int32, shape, len(shape) - 1) < HALF


def turn(values):
    return pltpu.roll(values, HALF, axis=values.ndim - 1)


def norm(values, mask=None):
    scale = 1.0 / values.shape[0]
    centred = values - jnp.sum(values, axis=0, keepdims=True) * scale
    factor = lax.rsqrt(jnp.sum(centred * centred, axis=0, keepdims=True) * scale + 1e-05)
    return centred * (factor if mask is None else factor * mask)


def dot(left, right, dims=((1,), (0,))):
    return lax.dot_general(left, right, (dims, ((), ())), preferred_element_type=F32)


def split(values):
    high = values.astype(BF16)
    return high, (values - high.astype(F32)).astype(BF16)


def halved(weights):
    rows = []
    for k in range(0, weights.shape[1], 128):
        high, low = split(weights[:, k : k + 128].T * 0.5)
        rows.append([jnp.concatenate([high, high], axis=1), jnp.concatenate([low, jnp.zeros_like(low)], axis=1)])
    if len(rows) == 1:
        return jnp.concatenate(rows[0], axis=0)
    return jnp.concatenate(rows[0] + rows[1][:1] + rows[2] + rows[3][:1] + rows[4][:1], axis=0)


def masks(tokens):
    row = lax.axis_index("row")
    col = lax.axis_index("col")
    line = tokens[pl.ds(col // 2, 1), :].astype(F32)
    pick = jnp.where(low_lanes((1, 128)), 1, 0) != col % 2
    cols = jnp.where(pick, line, turn(line))
    line = jnp.broadcast_to(tokens[pl.ds(row // 4, 1), :].astype(F32), (32, 128))
    lane = lax.broadcasted_iota(jnp.int32, (32, 128), 1)
    own = lax.broadcasted_iota(jnp.int32, (32, 128), 0) + 32 * (row % 4)
    rows = jnp.sum(jnp.where(lane == own, line, 0.0), axis=1, keepdims=True) * cols
    return jnp.where(low_lanes((TILES, 128)), rows[:TILES], rows[TILES:])


def mask_of(mask, tile):
    return jnp.concatenate([mask[tile : tile + 1], mask[tile + 1 : tile + 2]], axis=1)


def pair_tile(pair, tile):
    return pair[:, tile].reshape(128, 128).T


def sides(normed, weights, held, tile):
    both = jnp.concatenate(split(normed), axis=0)

    def side(k):
        linear = dot(weights[384 * k : 384 * (k + 1)], both)
        value = linear[:128] + linear[128:256]
        value = value + jnp.tanh(linear[256:]) * value
        for n in range(2):
            held[k, tile + n] = value[:, 128 * n : 128 * (n + 1)]

    side(0)
    side(1)
    return 1.0 + jnp.tanh(dot(weights[768:], both))


def pack(held, out):
    for side in range(2):
        for k in range(0, 128, 32):
            out[k : k + 32, 16 * side : 16 * side + 16, :] = jnp.swapaxes(held[side, :, k : k + 32, :], 0, 1).astype(BF16)


def project_kernel(token_h, pair_h, proj_h, out, flat, gating, mask, held, normed, tokens, pair, proj, semaphores):
    parts = [(slice(None), pl.ds(4 * k, 4)) for k in range(4)]
    copies = [
        pltpu.make_async_copy(pair_h.at[part], pair.at[part], semaphores.at[k])
        for k, part in enumerate(parts)
    ]
    weight_copy = pltpu.make_async_copy(proj_h, proj, semaphores.at[4])
    token_copy = pltpu.make_async_copy(token_h, tokens, semaphores.at[5])
    for copy in [token_copy] + copies[:2] + [weight_copy] + copies[2:]:
        copy.start()
    token_copy.wait()
    copies[0].wait()
    copies[1].wait()
    mask[...] = masks(tokens)
    for tile in range(0, TILES, 2):
        if tile == 8:
            weight_copy.wait()
            copies[2].wait()
            copies[3].wait()
            weights = halved(proj)
        lanes = slice(128 * tile, 128 * (tile + 2))
        values = jnp.concatenate([pair_tile(pair, tile), pair_tile(pair, tile + 1)], axis=1)
        flat[:, lanes] = values
        normed[:, lanes] = norm(values, mask_of(mask, tile))
    for tile in range(0, TILES, 2):
        lanes = slice(128 * tile, 128 * (tile + 2))
        gating[:, lanes] = sides(normed[:, lanes], weights, held, tile)
    pack(held, out)


def operands(got):
    matrices = []
    for side in range(2):
        halves = []
        for lanes in (slice(0, HALF), slice(HALF, 128)):
            parts = [got[:, k, 16 * side : 16 * side + 16, lanes] for k in range(8)]
            halves.append(jnp.concatenate(parts, axis=2))
        matrices.append(jnp.stack(halves, axis=1).reshape(512, 512))
    return matrices


def triangle_kernel(contract, got, out):
    left, right = operands(got)
    sums = dot(left, right, ((contract,), (contract,)))
    if contract == 1:
        sums = sums.astype(BF16)
    sums = sums.reshape(16, 2, 16, 512)
    low = low_lanes((16, 128))
    for n in range(16):
        for m in range(4):
            lanes = slice(128 * m, 128 * (m + 1))
            top, bottom = sums[n, 0, :, lanes], sums[n, 1, :, lanes]
            out[n, 2 * m] = jnp.where(low, top, turn(bottom)).astype(BF16)
            out[n, 2 * m + 1] = jnp.where(low, turn(top), bottom).astype(BF16)


def unpack(got):
    return jnp.swapaxes(got[...], 0, 1)


def finish(triangle, tile, flat, gating, closing):
    lanes = slice(128 * tile, 128 * (tile + 2))
    sums = jnp.concatenate([triangle[tile], triangle[tile + 1]], axis=1).astype(F32)
    product = dot(closing, jnp.concatenate(split(norm(sums)), axis=0))
    product = product[:128] + product[128:]
    return flat[:, lanes] + gating[:, lanes] * product


def middle_kernel(
    mask, got, flat, gating, final, proj, out, first, next_gating, held
):
    weights = halved(proj)
    closing = halved(final)
    triangle = unpack(got)
    for tile in range(0, TILES, 2):
        first[:, 128 * tile : 128 * (tile + 2)] = finish(triangle, tile, flat, gating, closing)
    for tile in range(0, TILES, 2):
        lanes = slice(128 * tile, 128 * (tile + 2))
        next_gating[:, lanes] = sides(norm(first[:, lanes], mask_of(mask, tile)), weights, held, tile)
    pack(held, out)


def last_kernel(got, first, gating, final, out, done, semaphores):
    closing = halved(final)
    triangle = unpack(got)
    copies = []
    for tile in range(0, TILES, 2):
        values = finish(triangle, tile, first, gating, closing)
        for k in range(2):
            part = values[:, 128 * k : 128 * (k + 1)].T
            done[tile + k] = part[:HALF]
            done[tile + k + 16] = part[HALF:]
        if tile % 4 == 2:
            for start in (tile - 2, tile + 14):
                rows = pl.ds(start, 4)
                copies.append(pltpu.make_async_copy(done.at[rows], out.at[rows], semaphores.at[len(copies)]))
                copies[-1].start()
    for copy in copies:
        copy.wait()


def shards(pair, token_mask, out_proj, out_final, in_proj, in_final):
    axes = ("row", "col")
    struct = jax.ShapeDtypeStruct
    lines = token_mask.reshape(4, 128)
    message = struct((128, 32, 128), BF16)
    answer = struct((16, 8, 16, 128), BF16)
    whole = struct((128, 2048), F32)
    held = pltpu.VMEM((2, TILES, 128, 128), F32)

    def swap(values):
        return lax.all_to_all(values, axes, 0, 0, tiled=True)

    def triangle(got, contract):
        kernel = functools.partial(triangle_kernel, contract)
        sums = call(kernel, answer, [], [VMEM], 2 * 512**3)(got.reshape(16, 8, 32, 128))
        return sums.reshape(128, 16, 128)

    scratch = [
        held,
        pltpu.VMEM((128, 2048), F32),
        pltpu.VMEM((4, 128), jnp.int32),
        pltpu.VMEM((2, TILES, HALF, 128), F32),
        pltpu.VMEM(out_proj.shape, F32),
        pltpu.SemaphoreType.DMA((6,)),
    ]
    sent, flat, gating, mask = call(
        project_kernel, (message, whole, whole, struct((TILES, 128), F32)), scratch, [HBM] * 3, 2 * 2048 * 128 * 640
    )(*[pltpu.with_memory_space_constraint(v, pltpu.HBM) for v in (lines, pair.reshape(2, TILES, HALF, 128), out_proj)])
    sums = swap(triangle(swap(sent), 1))
    sent, first, gating = call(
        middle_kernel, (message, whole, whole), [held], [VMEM] * 6, 2 * 2048 * 128 * 768
    )(mask, sums, flat, gating, out_final, in_proj)
    sums = swap(triangle(swap(sent), 0))
    return pl.pallas_call(
        last_kernel,
        out_shape=struct(pair.shape, F32),
        in_specs=[VMEM] * 4,
        out_specs=HBM,
        scratch_shapes=[pltpu.VMEM(pair.shape, F32), pltpu.SemaphoreType.DMA((8,))],
        compiler_params=pltpu.CompilerParams(vmem_limit_bytes=16 * 1024 * 1024),
        cost_estimate=pl.CostEstimate(flops=2 * 2048 * 128 * 128, bytes_accessed=3 << 20, transcendentals=0),
    )(sums, first, gating, in_final)


def solution(mesh):
    placed = (P("row", "col", None), P(), P(), P(), P(), P())
    return jax.shard_map(
        shards, mesh=mesh, in_specs=placed, out_specs=P("row", "col", None), check_vma=False
    )
```

```python
import functools

import jax
import jax.numpy as jnp
from jax import lax
from jax.experimental import pallas as pl
from jax.experimental.pallas import tpu as pltpu
from jax.sharding import PartitionSpec as P

HALF = 64
TILES = 16
F32 = jnp.float32
BF16 = jnp.bfloat16
VMEM = pl.BlockSpec(memory_space=pltpu.VMEM)
SMEM = pl.BlockSpec(memory_space=pltpu.SMEM)
HBM = pl.BlockSpec(memory_space=pltpu.HBM)


def call(kernel, outs, scratch, specs, flops, limit=16):
    return pl.pallas_call(
        kernel,
        out_shape=outs,
        in_specs=specs,
        out_specs=jax.tree.map(lambda _: VMEM, outs),
        scratch_shapes=scratch,
        compiler_params=pltpu.CompilerParams(vmem_limit_bytes=limit * 1024 * 1024),
        cost_estimate=pl.CostEstimate(flops=flops, bytes_accessed=3 << 20, transcendentals=1 << 19),
    )


def low_lanes(shape):
    return lax.broadcasted_iota(jnp.int32, shape, len(shape) - 1) < HALF


def turn(values):
    return pltpu.roll(values, HALF, axis=values.ndim - 1)


def norm(values, mask=None):
    scale = 1.0 / values.shape[0]
    centred = values - jnp.sum(values, axis=0, keepdims=True) * scale
    factor = lax.rsqrt(jnp.sum(centred * centred, axis=0, keepdims=True) * scale + 1e-05)
    return centred * (factor if mask is None else factor * mask)


def dot(left, right, dims=((1,), (0,))):
    return lax.dot_general(left, right, (dims, ((), ())), preferred_element_type=F32)


def split(values):
    high = values.astype(BF16)
    return high, (values - high.astype(F32)).astype(BF16)


def halved(weights):
    rows = []
    for k in range(0, weights.shape[1], 128):
        high, low = split(weights[:, k : k + 128].T * 0.5)
        rows.append([jnp.concatenate([high, high], axis=1), jnp.concatenate([low, jnp.zeros_like(low)], axis=1)])
    if len(rows) == 1:
        return jnp.concatenate(rows[0], axis=0)
    return jnp.concatenate(rows[0] + rows[1][:1] + rows[2] + rows[3][:1] + rows[4][:1], axis=0)


def masks(tokens):
    row = lax.axis_index("row")
    col = lax.axis_index("col")
    line = tokens[pl.ds(col // 2, 1), :].astype(F32)
    pick = jnp.where(low_lanes((1, 128)), 1, 0) != col % 2
    cols = jnp.where(pick, line, turn(line))
    line = jnp.broadcast_to(tokens[pl.ds(row // 4, 1), :].astype(F32), (32, 128))
    lane = lax.broadcasted_iota(jnp.int32, (32, 128), 1)
    own = lax.broadcasted_iota(jnp.int32, (32, 128), 0) + 32 * (row % 4)
    rows = jnp.sum(jnp.where(lane == own, line, 0.0), axis=1, keepdims=True) * cols
    return jnp.where(low_lanes((TILES, 128)), rows[:TILES], rows[TILES:])


def mask_of(mask, tile):
    return jnp.concatenate([mask[tile : tile + 1], mask[tile + 1 : tile + 2]], axis=1)


def pair_tile(pair, tile):
    return pair[:, tile].reshape(128, 128).T


def sides(normed, weights, held):
    both = jnp.concatenate(split(normed), axis=0)

    def side(k):
        linear = dot(weights[384 * k : 384 * (k + 1)], both)
        value = linear[:128] + linear[128:256]
        value = value + jnp.tanh(linear[256:]) * value
        for n in range(2):
            held[k].append(value[:, 128 * n : 128 * (n + 1)].astype(BF16))

    side(0)
    side(1)
    return 1.0 + jnp.tanh(dot(weights[768:], both))


def pack(held, out):
    for side in range(2):
        for k in range(0, 128, 32):
            out[k : k + 32, 16 * side : 16 * side + 16, :] = jnp.swapaxes(jnp.stack([part[k : k + 32] for part in held[side]]), 0, 1)


def project_kernel(token_h, pair_h, proj_h, out, flat, gating, mask, normed, tokens, pair, proj, semaphores):
    parts = [(slice(None), pl.ds(4 * k, 4)) for k in range(4)]
    copies = [
        pltpu.make_async_copy(pair_h.at[part], pair.at[part], semaphores.at[k])
        for k, part in enumerate(parts)
    ]
    weight_copy = pltpu.make_async_copy(proj_h, proj, semaphores.at[4])
    token_copy = pltpu.make_async_copy(token_h, tokens, semaphores.at[5])
    for copy in [token_copy] + copies[:2] + [weight_copy] + copies[2:]:
        copy.start()
    token_copy.wait()
    copies[0].wait()
    copies[1].wait()
    mask[...] = masks(tokens)
    for tile in range(0, TILES, 2):
        if tile == 8:
            weight_copy.wait()
            copies[2].wait()
            copies[3].wait()
            weights = halved(proj)
        lanes = slice(128 * tile, 128 * (tile + 2))
        values = jnp.concatenate([pair_tile(pair, tile), pair_tile(pair, tile + 1)], axis=1)
        flat[:, lanes] = values
        normed[:, lanes] = norm(values, mask_of(mask, tile))
    held = ([], [])
    for tile in range(0, TILES, 2):
        lanes = slice(128 * tile, 128 * (tile + 2))
        gating[:, lanes] = sides(normed[:, lanes], weights, held)
    pack(held, out)


def operands(got):
    matrices = []
    for side in range(2):
        halves = []
        for lanes in (slice(0, HALF), slice(HALF, 128)):
            parts = [got[:, k, 16 * side : 16 * side + 16, lanes] for k in range(8)]
            halves.append(jnp.concatenate(parts, axis=2))
        matrices.append(jnp.stack(halves, axis=1).reshape(512, 512))
    return matrices


def triangle_kernel(contract, got, out):
    left, right = operands(got)
    sums = dot(left, right, ((contract,), (contract,)))
    if contract == 1:
        sums = sums.astype(BF16)
    sums = sums.reshape(16, 2, 16, 512)
    low = low_lanes((16, 128))
    for n in range(16):
        for m in range(4):
            lanes = slice(128 * m, 128 * (m + 1))
            top, bottom = sums[n, 0, :, lanes], sums[n, 1, :, lanes]
            out[n, 2 * m] = jnp.where(low, top, turn(bottom)).astype(BF16)
            out[n, 2 * m + 1] = jnp.where(low, turn(top), bottom).astype(BF16)


def unpack(got):
    return jnp.swapaxes(got[...], 0, 1)


def finish(triangle, tile, flat, gating, closing):
    lanes = slice(128 * tile, 128 * (tile + 2))
    sums = jnp.concatenate([triangle[tile], triangle[tile + 1]], axis=1).astype(F32)
    product = dot(closing, jnp.concatenate(split(norm(sums)), axis=0))
    product = product[:128] + product[128:]
    return flat[:, lanes] + gating[:, lanes] * product


def middle_kernel(
    mask, got, flat, gating, final, proj, out, first, next_gating
):
    weights = halved(proj)
    closing = halved(final)
    triangle = unpack(got)
    for tile in range(0, TILES, 2):
        first[:, 128 * tile : 128 * (tile + 2)] = finish(triangle, tile, flat, gating, closing)
    held = ([], [])
    for tile in range(0, TILES, 2):
        lanes = slice(128 * tile, 128 * (tile + 2))
        next_gating[:, lanes] = sides(norm(first[:, lanes], mask_of(mask, tile)), weights, held)
    pack(held, out)


def last_kernel(got, first, gating, final, out, done, semaphores):
    closing = halved(final)
    triangle = unpack(got)
    copies = []
    for tile in range(0, TILES, 2):
        values = finish(triangle, tile, first, gating, closing)
        for k in range(2):
            part = values[:, 128 * k : 128 * (k + 1)].T
            done[tile + k] = part[:HALF]
            done[tile + k + 16] = part[HALF:]
        if tile % 4 == 2:
            for start in (tile - 2, tile + 14):
                rows = pl.ds(start, 4)
                copies.append(pltpu.make_async_copy(done.at[rows], out.at[rows], semaphores.at[len(copies)]))
                copies[-1].start()
    for copy in copies:
        copy.wait()


def shards(pair, token_mask, out_proj, out_final, in_proj, in_final):
    axes = ("row", "col")
    struct = jax.ShapeDtypeStruct
    lines = token_mask.reshape(4, 128)
    message = struct((128, 32, 128), BF16)
    answer = struct((16, 8, 16, 128), BF16)
    whole = struct((128, 2048), F32)

    def swap(values):
        return lax.all_to_all(values, axes, 0, 0, tiled=True)

    def triangle(got, contract):
        kernel = functools.partial(triangle_kernel, contract)
        sums = call(kernel, answer, [], [VMEM], 2 * 512**3)(got.reshape(16, 8, 32, 128))
        return sums.reshape(128, 16, 128)

    scratch = [
        pltpu.VMEM((128, 2048), F32),
        pltpu.VMEM((4, 128), jnp.int32),
        pltpu.VMEM((2, TILES, HALF, 128), F32),
        pltpu.VMEM(out_proj.shape, F32),
        pltpu.SemaphoreType.DMA((6,)),
    ]
    sent, flat, gating, mask = call(
        project_kernel, (message, whole, whole, struct((TILES, 128), F32)), scratch, [HBM] * 3, 2 * 2048 * 128 * 640
    )(*[pltpu.with_memory_space_constraint(v, pltpu.HBM) for v in (lines, pair.reshape(2, TILES, HALF, 128), out_proj)])
    sums = swap(triangle(swap(sent), 1))
    sent, first, gating = call(
        middle_kernel, (message, whole, whole), [], [VMEM] * 6, 2 * 2048 * 128 * 768
    )(mask, sums, flat, gating, out_final, in_proj)
    sums = swap(triangle(swap(sent), 0))
    return pl.pallas_call(
        last_kernel,
        out_shape=struct(pair.shape, F32),
        in_specs=[VMEM] * 4,
        out_specs=HBM,
        scratch_shapes=[pltpu.VMEM(pair.shape, F32), pltpu.SemaphoreType.DMA((8,))],
        compiler_params=pltpu.CompilerParams(vmem_limit_bytes=16 * 1024 * 1024),
        cost_estimate=pl.CostEstimate(flops=2 * 2048 * 128 * 128, bytes_accessed=3 << 20, transcendentals=0),
    )(sums, first, gating, in_final)


def solution(mesh):
    placed = (P("row", "col", None), P(), P(), P(), P(), P())
    return jax.shard_map(
        shards, mesh=mesh, in_specs=placed, out_specs=P("row", "col", None), check_vma=False
    )
```
